32 devices in a mesh: groups: 2 (over x), dap: 16 (over z, y, core).
Axes of the slice: x: 2, y: 2, z: 4, core: 2. Of those that a mesh axis runs over, the one named last changes fastest.
Arguments:
- pair: bfloat16 [640, 320, 128], P(('groups', 'dap')), parts along dimension 0, may hold values from -6 to 6
- d_out: bfloat16 [640, 320, 128], P(('groups', 'dap')), parts along dimension 0, may hold values from -6 to 6
- residue_mask: int32 [640], P('groups'), parts along dimension 0, may hold values from 0 to 1, as said below
- w_in: bfloat16 [128, 512], replicated, may hold values from -0.5 to 0.5
- w_gate: bfloat16 [128, 128], replicated, may hold values from -0.5 to 0.5
- w_out: bfloat16 [128, 128], replicated, may hold values from -0.5 to 0.5
Outputs:
- update: bfloat16 [640, 320, 128], P(('groups', 'dap')), parts along dimension 0
- d_pair: bfloat16 [640, 320, 128], P(('groups', 'dap')), parts along dimension 0
- d_w_in: float32 [256, 512], P('groups'), parts along dimension 0
- d_w_gate: float32 [256, 128], P('groups'), parts along dimension 0
- d_w_out: float32 [256, 128], P('groups'), parts along dimension 0
The draws below stay inside these ranges and needn't reach their ends.
There are 2 independent parts, one for each index of `groups`. The reference program is written for one: setup_inputs(seed, part) draws one part's arguments, and reference() takes and returns one part's arrays. A program takes and returns all parts, laid end to end along the dimension named above; an argument that names none is the same for every part. Nothing has to cross between parts.
Inputs may be any that keep to these rules, and one draw needn't show every extreme that they name: `residue_mask`: 1 for the first residues of a crop and 0 after them; at least 160 ones.
All inputs are finite; a program needn't handle non-finite values.
Results may differ from the reference program's by a relative error of at most 0.0089.
Values may be sent and summed in bfloat16 or wider, within the bound.
A program may use at most 192 MiB of HBM per device.

```python
import jax
import jax.numpy as jnp
from jax import lax

PAIR_CH = 128
HIDDEN_SIZE = 128
CROP = 320


def draw_residue_mask(key, part):
    key = jax.random.fold_in(key, 7)
    length = jax.random.randint(key, (), CROP // 2, CROP + 1)
    return (jnp.arange(CROP) < length).astype(jnp.int32)


def block_scale(stream_key, extent, shards, low, high):
    factor_of = 1.0
    for dim, shards_of in shards:
        steps = jax.random.uniform(jax.random.fold_in(jax.random.fold_in(stream_key, 6), dim), (shards_of,), jnp.float32, low / len(shards), high / len(shards))
        factor_of = factor_of * jnp.repeat(jnp.exp(steps), extent[dim] // shards_of).reshape((-1,) + (1,) * (len(extent) - 1 - dim))
    return factor_of


def noise(rng, dims, width, most, split=(), held_as=jnp.bfloat16):
    values = jax.random.normal(rng, dims, jnp.float32) * width
    if len(split) > 0:
        values = block_scale(rng, dims, split, -0.22, 0.18) * values
    return jnp.clip(values, min=-most, max=most).astype(held_as)


def setup_inputs(seed: int = 0, part: int = 0) -> dict:
    arg_keys = jax.random.split(jax.random.key(seed), 7)
    part_keys = jax.random.split(jax.random.fold_in(arg_keys[6], part), 7)
    pair = noise(part_keys[0], (CROP, CROP, PAIR_CH), 1.0, 6.0, ((0, 16),))
    d_out = noise(part_keys[1], (CROP, CROP, PAIR_CH), 1.0, 6.0, ((0, 16),))
    residue_mask = draw_residue_mask(jax.random.fold_in(jax.random.fold_in(arg_keys[6], part), 71), part)
    w_in = noise(arg_keys[3], (PAIR_CH, 4 * HIDDEN_SIZE), PAIR_CH ** -0.5, 0.5)
    w_gate = noise(arg_keys[4], (PAIR_CH, PAIR_CH), PAIR_CH ** -0.5, 0.5)
    w_out = noise(arg_keys[5], (HIDDEN_SIZE, PAIR_CH), HIDDEN_SIZE ** -0.5, 0.5)
    return dict(pair=pair, d_out=d_out, residue_mask=residue_mask, w_in=w_in, w_gate=w_gate, w_out=w_out)


def norm_axis(values, axis):
    center = values - lax.optimization_barrier(jnp.mean(values, axis=axis, keepdims=True))
    inverse = jax.lax.rsqrt(lax.optimization_barrier(jnp.mean(center * center, axis=axis, keepdims=True)) + 1e-05)
    return center * inverse

def norm_back(cotan, values, axis):
    center = values - lax.optimization_barrier(jnp.mean(values, axis=axis, keepdims=True))
    inverse = jax.lax.rsqrt(lax.optimization_barrier(jnp.mean(center * center, axis=axis, keepdims=True)) + 1e-05)
    normed = center * inverse
    shifted = cotan - lax.optimization_barrier(jnp.mean(cotan, axis=axis, keepdims=True))
    return inverse * (shifted - normed * lax.optimization_barrier(jnp.mean(cotan * normed, axis=axis, keepdims=True)))

def matmul(left_mat, right_mat):
    lead = left_mat.shape[:-1]
    flat = left_mat.reshape((-1, left_mat.shape[-1]))
    return jnp.dot(flat, right_mat, preferred_element_type=jnp.float32).reshape(lead + (right_mat.shape[-1],))

def weight_grad(first, second):
    flat_one = first.reshape((-1, first.shape[-1]))
    flat_two = second.reshape((-1, second.shape[-1]))
    return jnp.dot(flat_one.T, flat_two, preferred_element_type=jnp.float32)

def reference(pair, d_out, residue_mask, w_in, w_gate, w_out):
    pair_f = pair.astype(jnp.float32)
    normed = norm_axis(pair_f, -1).astype(jnp.bfloat16)
    mask_f = residue_mask.astype(jnp.float32)
    pmask = (mask_f[:, None] * mask_f[None, :])[:, :, None]
    lin_a = matmul(normed, w_in[:, 0:HIDDEN_SIZE])
    gate_a = matmul(normed, w_in[:, HIDDEN_SIZE:2 * HIDDEN_SIZE])
    lin_b = matmul(normed, w_in[:, 2 * HIDDEN_SIZE:3 * HIDDEN_SIZE])
    gate_b = matmul(normed, w_in[:, 3 * HIDDEN_SIZE:4 * HIDDEN_SIZE])
    sig_a = jax.nn.sigmoid(gate_a)
    sig_b = jax.nn.sigmoid(gate_b)
    left = (pmask * sig_a * lin_a).astype(jnp.bfloat16)
    right = (pmask * sig_b * lin_b).astype(jnp.bfloat16)
    tri = jnp.einsum('kih,kjh->ijh', left.astype(jnp.float32), right.astype(jnp.float32)).astype(jnp.bfloat16)
    tri_f = tri.astype(jnp.float32)
    tri_normed = norm_axis(tri_f, -1).astype(jnp.bfloat16)
    value = matmul(tri_normed, w_out)
    out_gate = jax.nn.sigmoid(matmul(normed, w_gate))
    update = (out_gate * value).astype(jnp.bfloat16)
    cot = d_out.astype(jnp.float32)
    d_value = (cot * out_gate).astype(jnp.bfloat16)
    d_gate_pre = (cot * value * out_gate * (1.0 - out_gate)).astype(jnp.bfloat16)
    d_tn = matmul(d_value, w_out.T)
    d_tri = norm_back(d_tn, tri_f, -1).astype(jnp.bfloat16)
    d_tri_f = d_tri.astype(jnp.float32)
    d_left = jnp.einsum('kjh,ijh->kih', right.astype(jnp.float32), d_tri_f).astype(jnp.bfloat16).astype(jnp.float32)
    d_right = jnp.einsum('kih,ijh->kjh', left.astype(jnp.float32), d_tri_f).astype(jnp.bfloat16).astype(jnp.float32)
    d_proj = jnp.concatenate([d_left * pmask * sig_a, d_left * pmask * lin_a * sig_a * (1.0 - sig_a), d_right * pmask * sig_b, d_right * pmask * lin_b * sig_b * (1.0 - sig_b)], axis=-1).astype(jnp.bfloat16)
    d_normed = matmul(d_proj, w_in.T) + matmul(d_gate_pre, w_gate.T)
    d_pair = norm_back(d_normed, pair_f, -1).astype(jnp.bfloat16)
    scale = jnp.float32(1.0 / CROP)
    d_w_in = weight_grad(normed, d_proj) * scale
    d_w_gate = weight_grad(normed, d_gate_pre) * scale
    d_w_out = weight_grad(tri_normed, d_value) * scale
    return (update, d_pair, d_w_in, d_w_gate, d_w_out)
```

```python
import functools
import math

import jax
import jax.numpy as jnp
from jax import lax
from jax.experimental import pallas as pl
from jax.experimental.pallas import tpu as pltpu
from jax.sharding import PartitionSpec as P

F32 = jnp.float32
BF16 = jnp.bfloat16
EPS = 1e-05
AXIS = "dap"


def greet(n):
    me = lax.axis_index(AXIS)
    barrier = pltpu.get_barrier_semaphore()

    def one(step, carry):
        peer = lax.rem(me + step, n)
        pl.semaphore_signal(barrier, inc=1, device_id={AXIS: peer}, device_id_type=pl.DeviceIdType.MESH)
        return carry

    lax.fori_loop(1, n, one, 0)
    pl.semaphore_wait(barrier, n - 1)


def push(src, dst, send_sem, recv_sem, peer):
    return pltpu.make_async_remote_copy(
        src_ref=src,
        dst_ref=dst,
        send_sem=send_sem,
        recv_sem=recv_sem,
        device_id={AXIS: peer},
        device_id_type=pl.DeviceIdType.MESH,
    )


def push_chunk(n, c, src, dst, send_sem, recv_sem):
    me = lax.axis_index(AXIS)

    def one(step, carry):
        peer = lax.rem(me + step, n)
        push(src.at[peer, c], dst.at[me, c], send_sem.at[c, peer], recv_sem.at[c, me], peer).start()
        return carry

    lax.fori_loop(1, n, one, 0)


def await_recv(n, c, src, dst, send_sem, recv_sem):
    me = lax.axis_index(AXIS)

    def one(step, carry):
        peer = lax.rem(me + n - step, n)
        push(src.at[peer, c], dst.at[peer, c], send_sem.at[c, peer], recv_sem.at[c, peer], peer).wait_recv()
        return carry

    lax.fori_loop(1, n, one, 0)


def await_send(n, c, src, dst, send_sem, recv_sem):
    me = lax.axis_index(AXIS)

    def one(step, carry):
        peer = lax.rem(me + step, n)
        push(src.at[peer, c], dst.at[me, c], send_sem.at[c, peer], recv_sem.at[c, me], peer).wait_send()
        return carry

    lax.fori_loop(1, n, one, 0)


def dot(a, b, da, db):
    return lax.dot_general(a, b, (((da,), (db,)), ((), ())), preferred_element_type=F32)


def loop(count, body):
    def step(c, carry):
        body(c)
        return carry

    lax.fori_loop(0, count, step, 0)


def first_kernel(n, chunks, group, pair_ref, mask_ref, w_ref, normed_ref, out_ref, send, send_sem, recv_sem, own_sem):
    me = lax.axis_index(AXIS)
    greet(n)
    half = w_ref.shape[0] // 2
    rows = half // n
    width = pair_ref.shape[1]

    def body(c):
        for j in range(group):
            q = c * group + j
            x = pair_ref[q].astype(F32)
            center = x - jnp.mean(x, axis=-1, keepdims=True)
            inverse = lax.rsqrt(jnp.mean(center * center, axis=-1, keepdims=True) + EPS)
            normed = (center * inverse).astype(BF16)
            normed_ref[q] = normed
            lin = dot(w_ref[0:half, :], normed, 1, 1)
            gate = dot(w_ref[half:, :], normed, 1, 1)
            gated = (mask_ref[q] * jax.nn.sigmoid(gate) * lin).reshape((n, rows, width))
            send[:, c, j * rows : (j + 1) * rows, :] = gated.astype(BF16)
        push_chunk(n, c, send, out_ref, send_sem, recv_sem)

    loop(chunks, body)
    own = pltpu.make_async_copy(send.at[me], out_ref.at[me], own_sem)
    own.start()
    loop(chunks, lambda c: await_send(n, c, send, out_ref, send_sem, recv_sem))
    loop(chunks, lambda c: await_recv(n, c, send, out_ref, send_sem, recv_sem))
    own.wait()


def middle_kernel(
    n, chunks, group,
    tri_ref, normed_ref, cotan_ref, w_gate_ref, w_out_ref,
    update_ref, dgp_ref, grad_ref, out_ref,
    recv, send, in_send_sem, in_recv_sem, send_sem, recv_sem, own_sem,
):
    me = lax.axis_index(AXIS)
    greet(n)
    loop(chunks, lambda c: push_chunk(n, c, tri_ref, recv, in_send_sem, in_recv_sem))
    own_in = pltpu.make_async_copy(tri_ref.at[me], recv.at[me], own_sem.at[0])
    own_in.start()
    hidden = w_out_ref.shape[0]
    rows = hidden // n
    width = normed_ref.shape[1]
    grad_ref[...] = jnp.zeros_like(grad_ref)
    own_in.wait()

    def body(c):
        await_recv(n, c, tri_ref, recv, in_send_sem, in_recv_sem)
        block = recv[:, c].astype(F32)
        parts = []
        for j in range(group):
            q = c * group + j
            tri = block[:, j * rows : (j + 1) * rows, :].reshape((hidden, width))
            center = tri - jnp.mean(tri, axis=0, keepdims=True)
            inverse = lax.rsqrt(jnp.mean(center * center, axis=0, keepdims=True) + EPS)
            hat = center * inverse
            tri_normed = hat.astype(BF16)
            value = dot(tri_normed, w_out_ref[...], 0, 0)
            normed = normed_ref[q]
            out_gate = jax.nn.sigmoid(dot(normed, w_gate_ref[...], 1, 0))
            cotan = cotan_ref[q].astype(F32)
            update_ref[q] = (out_gate * value).astype(BF16)
            d_value = (cotan * out_gate).astype(BF16)
            dgp = (cotan * value * out_gate * (1.0 - out_gate)).astype(BF16)
            dgp_ref[q] = dgp
            grad_ref[0:hidden, :] += dot(tri_normed, d_value, 1, 0)
            grad_ref[hidden:, :] += dot(normed, dgp, 0, 0)
            d_tn = dot(w_out_ref[...], d_value, 1, 1)
            shifted = d_tn - jnp.mean(d_tn, axis=0, keepdims=True)
            d_tri = inverse * (shifted - hat * jnp.mean(d_tn * hat, axis=0, keepdims=True))
            parts.append(d_tri.reshape((n, rows, width)))
        send[:, c] = jnp.concatenate(parts, axis=1).astype(BF16)
        push_chunk(n, c, send, out_ref, send_sem, recv_sem)

    loop(chunks, body)
    own = pltpu.make_async_copy(send.at[me], out_ref.at[me], own_sem.at[1])
    own.start()
    loop(chunks, lambda c: await_send(n, c, tri_ref, recv, in_send_sem, in_recv_sem))
    loop(chunks, lambda c: await_send(n, c, send, out_ref, send_sem, recv_sem))
    loop(chunks, lambda c: await_recv(n, c, send, out_ref, send_sem, recv_sem))
    own.wait()


def last_kernel(
    n, chunks, group, scale,
    dlr_ref, pair_ref, normed_ref, dgp_ref, mask_ref, w_t_ref, w_ref, w_gate_ref, grad_ref,
    d_pair_ref, total_ref,
    recv, grads, slices, in_send_sem, in_recv_sem, rs_send, rs_recv, ag_send, ag_recv, own_sem,
):
    me = lax.axis_index(AXIS)
    greet(n)
    loop(chunks, lambda c: push_chunk(n, c, dlr_ref, recv, in_send_sem, in_recv_sem))
    own_in = pltpu.make_async_copy(dlr_ref.at[me], recv.at[me], own_sem)
    own_in.start()
    full = w_t_ref.shape[0]
    half = full // 2
    rows = half // n
    width = pair_ref.shape[1]
    part = slices.shape[1]
    channels = w_ref.shape[0]
    own_in.wait()

    def body(c):
        await_recv(n, c, dlr_ref, recv, in_send_sem, in_recv_sem)
        block = recv[:, c].astype(F32)
        for j in range(group):
            q = c * group + j
            cotan = block[:, j * rows : (j + 1) * rows, :].reshape((half, width)) * mask_ref[q]
            normed = normed_ref[q]
            lin = dot(w_t_ref[0:half, :], normed, 1, 1)
            sig = jax.nn.sigmoid(dot(w_t_ref[half:, :], normed, 1, 1))
            d_lin = cotan * sig
            d_gate = (d_lin * lin * (1.0 - sig)).astype(BF16)
            d_lin = d_lin.astype(BF16)
            grads[0:half, :] += dot(d_lin, normed, 1, 0)
            grads[half:full, :] += dot(d_gate, normed, 1, 0)
            d_normed = dot(w_ref[:, 0:half], d_lin, 1, 0) + dot(w_ref[:, half:], d_gate, 1, 0)
            d_normed = d_normed.T + dot(dgp_ref[q], w_gate_ref[...], 1, 1)
            x = pair_ref[q].astype(F32)
            center = x - jnp.mean(x, axis=-1, keepdims=True)
            inverse = lax.rsqrt(jnp.mean(center * center, axis=-1, keepdims=True) + EPS)
            hat = center * inverse
            shifted = d_normed - jnp.mean(d_normed, axis=-1, keepdims=True)
            d_pair = inverse * (shifted - hat * jnp.mean(d_normed * hat, axis=-1, keepdims=True))
            d_pair_ref[q] = d_pair.astype(BF16)

    grads[0:full, :] = jnp.zeros((full, channels), F32)
    grads[full:, :] = grad_ref[...]
    loop(chunks, body)

    def own_rows(d):
        return grads.at[pl.ds(pl.multiple_of(d * part, 8), part), :]

    def scatter(step, carry):
        peer = lax.rem(me + step, n)
        push(own_rows(peer), slices.at[me], rs_send.at[peer], rs_recv.at[me], peer).start()
        return carry

    lax.fori_loop(1, n, scatter, 0)
    slices[me] = grads[pl.ds(pl.multiple_of(me * part, 8), part), :]

    def scattered(step, carry):
        peer = lax.rem(me + n - step, n)
        push(own_rows(peer), slices.at[peer], rs_send.at[peer], rs_recv.at[peer], peer).wait_recv()
        return carry

    lax.fori_loop(1, n, scattered, 0)
    total = slices[0]
    for d in range(1, n):
        total = total + slices[d]
    total_ref[me] = total * scale

    def gather(step, carry):
        peer = lax.rem(me + step, n)
        push(total_ref.at[me], total_ref.at[me], ag_send.at[peer], ag_recv.at[me], peer).start()
        return carry

    lax.fori_loop(1, n, gather, 0)

    def gathered(step, carry):
        peer = lax.rem(me + n - step, n)
        push(total_ref.at[me], total_ref.at[peer], ag_send.at[peer], ag_recv.at[peer], peer).wait_recv()
        return carry

    lax.fori_loop(1, n, gathered, 0)

    def sent(step, carry):
        peer = lax.rem(me + step, n)
        push(own_rows(peer), slices.at[me], rs_send.at[peer], rs_recv.at[me], peer).wait_send()
        push(total_ref.at[me], total_ref.at[me], ag_send.at[peer], ag_recv.at[me], peer).wait_send()
        return carry

    lax.fori_loop(1, n, sent, 0)
    loop(chunks, lambda c: await_send(n, c, dlr_ref, recv, in_send_sem, in_recv_sem))


VMEM = pl.BlockSpec(memory_space=pltpu.VMEM)
ANY = pl.BlockSpec(memory_space=pl.ANY)
DMA = pltpu.SemaphoreType.DMA


def params(which):
    return pltpu.CompilerParams(collective_id=which, has_side_effects=True, vmem_limit_bytes=50 * 1024 * 1024)


def shards(n, pair, d_out, residue_mask, w_in, w_gate, w_out):
    row_count, crop, channels = pair.shape
    hidden = w_out.shape[0]
    hd = hidden // n
    fold = 128 // math.gcd(128, crop)
    width = fold * crop
    steps = row_count // fold
    me = lax.axis_index(AXIS)
    mask_all = residue_mask.astype(F32)
    mask_rows = lax.dynamic_slice_in_dim(mask_all, me * row_count, row_count, 0)
    pmask = (mask_rows[:, None] * mask_all[None, :]).reshape((steps, 1, width))
    w_perm = w_in.reshape((channels, 2, 2, n, hd)).transpose((0, 2, 3, 1, 4)).reshape((channels, 4 * hidden))
    w_perm_t = w_perm.T
    pair_q = pair.reshape((steps, width, channels))
    cotan_q = d_out.reshape((steps, width, channels))

    group = 32 // (2 * hd)
    chunks = steps // group
    lr_shape = (n, chunks, group * 2 * hd, width)
    normed, lr = pl.pallas_call(
        functools.partial(first_kernel, n, chunks, group),
        name="project_and_send",
        out_shape=(
            jax.ShapeDtypeStruct((steps, width, channels), BF16),
            jax.ShapeDtypeStruct(lr_shape, BF16),
        ),
        in_specs=[VMEM] * 3,
        out_specs=(VMEM, ANY),
        scratch_shapes=[pltpu.VMEM(lr_shape, BF16), DMA((chunks, n)), DMA((chunks, n)), DMA],
        compiler_params=params(0),
    )(pair_q, pmask, w_perm_t)

    lr = lr.reshape((n, steps, 2, hd, fold, crop)).transpose((2, 3, 0, 1, 4, 5)).reshape((2, hd, n * row_count, crop))
    left, right = lr[0], lr[1]
    tri = jnp.einsum("hki,hkj->hij", left, right, preferred_element_type=F32).astype(BF16)
    group3 = 16 // hd
    chunks3 = steps // group3
    tri_shape = (n, chunks3, group3 * hd, width)
    tri = tri.reshape((hd, n, steps, fold, crop)).transpose((1, 2, 0, 3, 4)).reshape(tri_shape)

    update, dgp, grads, d_tri = pl.pallas_call(
        functools.partial(middle_kernel, n, chunks3, group3),
        name="gate_and_back",
        out_shape=(
            jax.ShapeDtypeStruct((steps, width, channels), BF16),
            jax.ShapeDtypeStruct((steps, width, channels), BF16),
            jax.ShapeDtypeStruct((hidden + channels, channels), F32),
            jax.ShapeDtypeStruct(tri_shape, BF16),
        ),
        in_specs=[ANY] + [VMEM] * 4,
        out_specs=(VMEM, VMEM, VMEM, ANY),
        scratch_shapes=[
            pltpu.VMEM(tri_shape, BF16),
            pltpu.VMEM(tri_shape, BF16),
            DMA((chunks3, n)),
            DMA((chunks3, n)),
            DMA((chunks3, n)),
            DMA((chunks3, n)),
            DMA((2,)),
        ],
        compiler_params=params(1),
    )(tri, normed, cotan_q, w_gate, w_out)

    d_tri = d_tri.reshape((n, steps, hd, fold, crop)).transpose((2, 0, 1, 3, 4)).reshape((hd, n * row_count, crop))
    d_left = jnp.einsum("hkj,hij->hki", right, d_tri, preferred_element_type=F32).astype(BF16)
    d_right = jnp.einsum("hki,hij->hkj", left, d_tri, preferred_element_type=F32).astype(BF16)
    dlr = jnp.stack([d_left, d_right]).reshape((2, hd, n, steps, fold, crop))
    dlr = dlr.transpose((2, 3, 0, 1, 4, 5)).reshape(lr_shape)

    grad_rows = 4 * hidden + hidden + channels
    part = grad_rows // n
    d_pair, total = pl.pallas_call(
        functools.partial(last_kernel, n, chunks, group, 1.0 / crop),
        name="pair_gradient",
        out_shape=(
            jax.ShapeDtypeStruct((steps, width, channels), BF16),
            jax.ShapeDtypeStruct((n, part, channels), F32),
        ),
        in_specs=[ANY] + [VMEM] * 8,
        out_specs=(VMEM, VMEM),
        scratch_shapes=[
            pltpu.VMEM(lr_shape, BF16),
            pltpu.VMEM((grad_rows, channels), F32),
            pltpu.VMEM((n, part, channels), F32),
            DMA((chunks, n)),
            DMA((chunks, n)),
            DMA((n,)),
            DMA((n,)),
            DMA((n,)),
            DMA((n,)),
            DMA,
        ],
        compiler_params=params(2),
    )(dlr, pair_q, normed, dgp, pmask, w_perm_t, w_perm, w_gate, grads)

    total = total.reshape((grad_rows, channels))
    total_in = total[: 4 * hidden].reshape((2, n, 2, hd, channels)).transpose((4, 2, 0, 1, 3))
    total_in = total_in.reshape((channels, 4 * hidden))
    return (
        update.reshape(pair.shape),
        d_pair.reshape(pair.shape),
        total_in,
        total[5 * hidden :],
        total[4 * hidden : 5 * hidden],
    )


def solution(mesh):
    in_specs = (
        P(("groups", "dap"), None, None),
        P(("groups", "dap"), None, None),
        P("groups"),
        P(),
        P(),
        P(),
    )
    out_specs = (
        P(("groups", "dap"), None, None),
        P(("groups", "dap"), None, None),
        P("groups", None),
        P("groups", None),
        P("groups", None),
    )
    body = functools.partial(shards, mesh.shape[AXIS])
    return jax.shard_map(body, mesh=mesh, in_specs=in_specs, out_specs=out_specs, check_vma=False)
```

```python
import functools
import math

import jax
import jax.numpy as jnp
from jax import lax
from jax.experimental import pallas as pl
from jax.experimental.pallas import tpu as pltpu
from jax.sharding import PartitionSpec as P

F32 = jnp.float32
BF16 = jnp.bfloat16
EPS = 1e-05
AXIS = "dap"
LANES = 128


def greet(n):
    me = lax.axis_index(AXIS)
    barrier = pltpu.get_barrier_semaphore()

    def one(step, carry):
        peer = lax.rem(me + step, n)
        pl.semaphore_signal(barrier, inc=1, device_id={AXIS: peer}, device_id_type=pl.DeviceIdType.MESH)
        return carry

    lax.fori_loop(1, n, one, 0)
    pl.semaphore_wait(barrier, n - 1)


def push(src, dst, send_sem, recv_sem, peer):
    return pltpu.make_async_remote_copy(
        src_ref=src,
        dst_ref=dst,
        send_sem=send_sem,
        recv_sem=recv_sem,
        device_id={AXIS: peer},
        device_id_type=pl.DeviceIdType.MESH,
    )


def push_chunk(n, c, src, dst, send_sem, recv_sem):
    me = lax.axis_index(AXIS)

    def one(step, carry):
        peer = lax.rem(me + step, n)
        push(src.at[peer, c], dst.at[me, c], send_sem.at[c, peer], recv_sem.at[c, me], peer).start()
        return carry

    lax.fori_loop(1, n, one, 0)


def await_recv(n, c, src, dst, send_sem, recv_sem):
    me = lax.axis_index(AXIS)

    def one(step, carry):
        peer = lax.rem(me + n - step, n)
        push(src.at[peer, c], dst.at[peer, c], send_sem.at[c, peer], recv_sem.at[c, peer], peer).wait_recv()
        return carry

    lax.fori_loop(1, n, one, 0)


def await_send(n, c, src, dst, send_sem, recv_sem):
    me = lax.axis_index(AXIS)

    def one(step, carry):
        peer = lax.rem(me + step, n)
        push(src.at[peer, c], dst.at[me, c], send_sem.at[c, peer], recv_sem.at[c, me], peer).wait_send()
        return carry

    lax.fori_loop(1, n, one, 0)


def dot(a, b, da, db):
    return lax.dot_general(a, b, (((da,), (db,)), ((), ())), preferred_element_type=F32)


def loop(count, body):
    def step(c, carry):
        body(c)
        return carry

    lax.fori_loop(0, count, step, 0)


def first_kernel(n, chunks, group, pair_ref, mask_ref, w_ref, normed_ref, out_ref, send, send_sem, recv_sem, own_sem):
    me = lax.axis_index(AXIS)
    greet(n)
    half = w_ref.shape[0] // 2
    rows = half // n
    width = pair_ref.shape[1]

    def body(c):
        for j in range(group):
            q = c * group + j
            x = pair_ref[q].astype(F32)
            center = x - jnp.mean(x, axis=-1, keepdims=True)
            inverse = lax.rsqrt(jnp.mean(center * center, axis=-1, keepdims=True) + EPS)
            normed = (center * inverse).astype(BF16)
            normed_ref[q] = normed
            lin = dot(w_ref[0:half, :], normed, 1, 1)
            gate = dot(w_ref[half:, :], normed, 1, 1)
            gated = (mask_ref[q] * jax.nn.sigmoid(gate) * lin).reshape((n, rows, width))
            send[:, c, j * rows : (j + 1) * rows, :] = gated.astype(BF16)
        push_chunk(n, c, send, out_ref, send_sem, recv_sem)

    loop(chunks, body)
    own = pltpu.make_async_copy(send.at[me], out_ref.at[me], own_sem)
    own.start()
    loop(chunks, lambda c: await_send(n, c, send, out_ref, send_sem, recv_sem))
    loop(chunks, lambda c: await_recv(n, c, send, out_ref, send_sem, recv_sem))
    own.wait()


def middle_kernel(
    n, chunks, group,
    tri_ref, normed_ref, cotan_ref, w_gate_ref, w_out_ref,
    update_ref, dgp_ref, grad_ref, out_ref,
    recv, send, in_send_sem, in_recv_sem, send_sem, recv_sem, own_sem,
):
    me = lax.axis_index(AXIS)
    greet(n)
    loop(chunks, lambda c: push_chunk(n, c, tri_ref, recv, in_send_sem, in_recv_sem))
    own_in = pltpu.make_async_copy(tri_ref.at[me], recv.at[me], own_sem.at[0])
    own_in.start()
    hidden = w_out_ref.shape[0]
    rows = hidden // n
    width = normed_ref.shape[1]
    grad_ref[...] = jnp.zeros_like(grad_ref)
    own_in.wait()

    def body(c):
        await_recv(n, c, tri_ref, recv, in_send_sem, in_recv_sem)
        block = recv[:, c].astype(F32)
        parts = []
        for j in range(group):
            q = c * group + j
            tri = block[:, j * rows : (j + 1) * rows, :].reshape((hidden, width))
            center = tri - jnp.mean(tri, axis=0, keepdims=True)
            inverse = lax.rsqrt(jnp.mean(center * center, axis=0, keepdims=True) + EPS)
            hat = center * inverse
            tri_normed = hat.astype(BF16)
            value = dot(tri_normed, w_out_ref[...], 0, 0)
            normed = normed_ref[q]
            out_gate = jax.nn.sigmoid(dot(normed, w_gate_ref[...], 1, 0))
            cotan = cotan_ref[q].astype(F32)
            update_ref[q] = (out_gate * value).astype(BF16)
            d_value = (cotan * out_gate).astype(BF16)
            dgp = (cotan * value * out_gate * (1.0 - out_gate)).astype(BF16)
            dgp_ref[q] = dgp
            grad_ref[0:hidden, :] += dot(tri_normed, d_value, 1, 0)
            grad_ref[hidden:, :] += dot(normed, dgp, 0, 0)
            d_tn = dot(w_out_ref[...], d_value, 1, 1)
            shifted = d_tn - jnp.mean(d_tn, axis=0, keepdims=True)
            d_tri = inverse * (shifted - hat * jnp.mean(d_tn * hat, axis=0, keepdims=True))
            parts.append(d_tri.reshape((n, rows, width)))
        send[:, c] = jnp.concatenate(parts, axis=1).astype(BF16)
        push_chunk(n, c, send, out_ref, send_sem, recv_sem)

    loop(chunks, body)
    own = pltpu.make_async_copy(send.at[me], out_ref.at[me], own_sem.at[1])
    own.start()
    loop(chunks, lambda c: await_send(n, c, tri_ref, recv, in_send_sem, in_recv_sem))
    loop(chunks, lambda c: await_send(n, c, send, out_ref, send_sem, recv_sem))
    loop(chunks, lambda c: await_recv(n, c, send, out_ref, send_sem, recv_sem))
    own.wait()


def last_kernel(
    n, chunks, group, scale,
    dlr_ref, pair_ref, normed_ref, dgp_ref, mask_ref, w_t_ref, w_ref, w_gate_ref, grad_ref,
    d_pair_ref, total_ref,
    recv, grads, slices, in_send_sem, in_recv_sem, rs_send, rs_recv, ag_send, ag_recv, own_sem,
):
    me = lax.axis_index(AXIS)
    greet(n)
    loop(chunks, lambda c: push_chunk(n, c, dlr_ref, recv, in_send_sem, in_recv_sem))
    own_in = pltpu.make_async_copy(dlr_ref.at[me], recv.at[me], own_sem)
    own_in.start()
    full = w_t_ref.shape[0]
    half = full // 2
    rows = half // n
    width = pair_ref.shape[1]
    part = slices.shape[1]
    channels = w_ref.shape[0]
    own_in.wait()

    def body(c):
        await_recv(n, c, dlr_ref, recv, in_send_sem, in_recv_sem)
        block = recv[:, c].astype(F32)
        for j in range(group):
            q = c * group + j
            cotan = block[:, j * rows : (j + 1) * rows, :].reshape((half, width)) * mask_ref[q]
            normed = normed_ref[q]
            lin = dot(w_t_ref[0:half, :], normed, 1, 1)
            sig = jax.nn.sigmoid(dot(w_t_ref[half:, :], normed, 1, 1))
            d_lin = cotan * sig
            d_gate = (d_lin * lin * (1.0 - sig)).astype(BF16)
            d_lin = d_lin.astype(BF16)
            grads[0:half, :] += dot(d_lin, normed, 1, 0)
            grads[half:full, :] += dot(d_gate, normed, 1, 0)
            d_normed = dot(w_ref[:, 0:half], d_lin, 1, 0) + dot(w_ref[:, half:], d_gate, 1, 0)
            d_normed = d_normed.T + dot(dgp_ref[q], w_gate_ref[...], 1, 1)
            x = pair_ref[q].astype(F32)
            center = x - jnp.mean(x, axis=-1, keepdims=True)
            inverse = lax.rsqrt(jnp.mean(center * center, axis=-1, keepdims=True) + EPS)
            hat = center * inverse
            shifted = d_normed - jnp.mean(d_normed, axis=-1, keepdims=True)
            d_pair = inverse * (shifted - hat * jnp.mean(d_normed * hat, axis=-1, keepdims=True))
            d_pair_ref[q] = d_pair.astype(BF16)

    grads[0:full, :] = jnp.zeros((full, channels), F32)
    grads[full:, :] = grad_ref[...]
    loop(chunks, body)

    def own_rows(d):
        return grads.at[pl.ds(pl.multiple_of(d * part, 8), part), :]

    def scatter(step, carry):
        peer = lax.rem(me + step, n)
        push(own_rows(peer), slices.at[me], rs_send.at[peer], rs_recv.at[me], peer).start()
        return carry

    lax.fori_loop(1, n, scatter, 0)
    slices[me] = grads[pl.ds(pl.multiple_of(me * part, 8), part), :]

    def scattered(step, carry):
        peer = lax.rem(me + n - step, n)
        push(own_rows(peer), slices.at[peer], rs_send.at[peer], rs_recv.at[peer], peer).wait_recv()
        return carry

    lax.fori_loop(1, n, scattered, 0)
    total = slices[0]
    for d in range(1, n):
        total = total + slices[d]
    total_ref[me] = total * scale

    def gather(step, carry):
        peer = lax.rem(me + step, n)
        push(total_ref.at[me], total_ref.at[me], ag_send.at[peer], ag_recv.at[me], peer).start()
        return carry

    lax.fori_loop(1, n, gather, 0)

    def gathered(step, carry):
        peer = lax.rem(me + n - step, n)
        push(total_ref.at[me], total_ref.at[peer], ag_send.at[peer], ag_recv.at[peer], peer).wait_recv()
        return carry

    lax.fori_loop(1, n, gathered, 0)

    def sent(step, carry):
        peer = lax.rem(me + step, n)
        push(own_rows(peer), slices.at[me], rs_send.at[peer], rs_recv.at[me], peer).wait_send()
        push(total_ref.at[me], total_ref.at[me], ag_send.at[peer], ag_recv.at[me], peer).wait_send()
        return carry

    lax.fori_loop(1, n, sent, 0)
    loop(chunks, lambda c: await_send(n, c, dlr_ref, recv, in_send_sem, in_recv_sem))


def take(ref, start, count, stride):
    return jnp.concatenate([ref[t, pl.ds(start, count, stride=stride), :] for t in range(ref.shape[0])], axis=1)


def put(ref, start, count, stride, values):
    short = ref.shape[0] * LANES - values.shape[1]
    if short:
        values = jnp.concatenate([values, jnp.zeros((values.shape[0], short), values.dtype)], axis=1)
    for t in range(ref.shape[0]):
        ref[t, pl.ds(start, count, stride=stride), :] = values[:, t * LANES : (t + 1) * LANES]


def unfold(wide, start, stride, fold):
    block = take(wide, start, wide.shape[1] // stride, stride).astype(BF16)
    crop = block.shape[1] // fold
    return jnp.concatenate([block[:, f * crop : (f + 1) * crop] for f in range(fold)], axis=0)


def refold(values, fold):
    count = values.shape[0] // fold
    return jnp.concatenate([values[f * count : (f + 1) * count, :] for f in range(fold)], axis=1)


def widen(n, src, wide):
    size = src.shape[1] * src.shape[2]

    def one(d):
        block = src[d].astype(F32).reshape((size, src.shape[3]))
        for t in range(wide.shape[0]):
            wide[t, pl.ds(pl.multiple_of(d * size, 8), size), :] = block[:, t * LANES : (t + 1) * LANES]

    loop(n, one)


def narrow(n, wide, dst):
    size = dst.shape[1] * dst.shape[2]

    def one(d):
        parts = [wide[t, pl.ds(pl.multiple_of(d * size, 8), size), :] for t in range(wide.shape[0])]
        dst[d] = jnp.concatenate(parts, axis=1).reshape(dst.shape[1:]).astype(BF16)

    loop(n, one)


def triangle_kernel(n, hd, fold, lr_ref, tri_ref, sides_ref, wide, rows, wire):
    widen(n, lr_ref, wide)
    count = wire.shape[1] // hd
    crop = sides_ref.shape[3]
    for h in range(hd):
        left = unfold(wide, h, 2 * hd, fold)
        right = unfold(wide, hd + h, 2 * hd, fold)
        sides_ref[0, h] = left
        sides_ref[1, h] = right
        put(rows, 0, count * fold, 1, dot(left, right, 0, 0))
        parts = [take(rows, f, count, fold)[:, :crop] for f in range(fold)]
        put(wire, h, count, hd, jnp.concatenate(parts, axis=1))
    narrow(n, wire, tri_ref)


def triangle_back_kernel(n, hd, fold, d_tri_ref, sides_ref, dlr_ref, wide, rows, wire):
    widen(n, d_tri_ref, wire)
    count = wire.shape[1] // hd
    crop = sides_ref.shape[3]
    for h in range(hd):
        block = take(wire, h, count, hd)
        for f in range(fold):
            put(rows, f, count, fold, block[:, f * crop : (f + 1) * crop])
        d_tri = take(rows, 0, count * fold, 1)[:, :crop].astype(BF16)
        d_left = dot(sides_ref[1, h], d_tri, 1, 1)
        d_right = dot(sides_ref[0, h], d_tri, 1, 0)
        put(wide, h, count, 2 * hd, refold(d_left, fold))
        put(wide, hd + h, count, 2 * hd, refold(d_right, fold))
    narrow(n, wide, dlr_ref)


VMEM = pl.BlockSpec(memory_space=pltpu.VMEM)
ANY = pl.BlockSpec(memory_space=pl.ANY)
DMA = pltpu.SemaphoreType.DMA


def params(which):
    return pltpu.CompilerParams(collective_id=which, has_side_effects=True, vmem_limit_bytes=50 * 1024 * 1024)


def shards(n, pair, d_out, residue_mask, w_in, w_gate, w_out):
    row_count, crop, channels = pair.shape
    hidden = w_out.shape[0]
    hd = hidden // n
    fold = 128 // math.gcd(128, crop)
    width = fold * crop
    steps = row_count // fold
    me = lax.axis_index(AXIS)
    mask_all = residue_mask.astype(F32)
    mask_rows = lax.dynamic_slice_in_dim(mask_all, me * row_count, row_count, 0)
    pmask = (mask_rows[:, None] * mask_all[None, :]).reshape((steps, 1, width))
    w_perm = w_in.reshape((channels, 2, 2, n, hd)).transpose((0, 2, 3, 1, 4)).reshape((channels, 4 * hidden))
    w_perm_t = w_perm.T
    pair_q = pair.reshape((steps, width, channels))
    cotan_q = d_out.reshape((steps, width, channels))

    group = 32 // (2 * hd)
    chunks = steps // group
    lr_shape = (n, chunks, group * 2 * hd, width)
    normed, lr = pl.pallas_call(
        functools.partial(first_kernel, n, chunks, group),
        name="project_and_send",
        out_shape=(
            jax.ShapeDtypeStruct((steps, width, channels), BF16),
            jax.ShapeDtypeStruct(lr_shape, BF16),
        ),
        in_specs=[VMEM] * 3,
        out_specs=(VMEM, ANY),
        scratch_shapes=[pltpu.VMEM(lr_shape, BF16), DMA((chunks, n)), DMA((chunks, n)), DMA],
        compiler_params=params(0),
    )(pair_q, pmask, w_perm_t)

    group3 = 16 // hd
    chunks3 = steps // group3
    tri_shape = (n, chunks3, group3 * hd, width)
    crop_rows = n * row_count
    relayout = [
        pltpu.VMEM((width // LANES, n * steps * 2 * hd, LANES), F32),
        pltpu.VMEM(((crop + LANES - 1) // LANES, crop_rows, LANES), F32),
        pltpu.VMEM((width // LANES, n * steps * hd, LANES), F32),
    ]
    tri, sides = pl.pallas_call(
        functools.partial(triangle_kernel, n, hd, fold),
        name="triangle",
        out_shape=(
            jax.ShapeDtypeStruct(tri_shape, BF16),
            jax.ShapeDtypeStruct((2, hd, crop_rows, crop), BF16),
        ),
        in_specs=[VMEM],
        out_specs=(VMEM, VMEM),
        scratch_shapes=relayout,
        compiler_params=pltpu.CompilerParams(vmem_limit_bytes=50 * 1024 * 1024),
    )(lr)

    update, dgp, grads, d_tri = pl.pallas_call(
        functools.partial(middle_kernel, n, chunks3, group3),
        name="gate_and_back",
        out_shape=(
            jax.ShapeDtypeStruct((steps, width, channels), BF16),
            jax.ShapeDtypeStruct((steps, width, channels), BF16),
            jax.ShapeDtypeStruct((hidden + channels, channels), F32),
            jax.ShapeDtypeStruct(tri_shape, BF16),
        ),
        in_specs=[ANY] + [VMEM] * 4,
        out_specs=(VMEM, VMEM, VMEM, ANY),
        scratch_shapes=[
            pltpu.VMEM(tri_shape, BF16),
            pltpu.VMEM(tri_shape, BF16),
            DMA((chunks3, n)),
            DMA((chunks3, n)),
            DMA((chunks3, n)),
            DMA((chunks3, n)),
            DMA((2,)),
        ],
        compiler_params=params(1),
    )(tri, normed, cotan_q, w_gate, w_out)

    dlr = pl.pallas_call(
        functools.partial(triangle_back_kernel, n, hd, fold),
        name="triangle_back",
        out_shape=jax.ShapeDtypeStruct(lr_shape, BF16),
        in_specs=[VMEM, VMEM],
        out_specs=VMEM,
        scratch_shapes=relayout,
        compiler_params=pltpu.CompilerParams(vmem_limit_bytes=50 * 1024 * 1024),
    )(d_tri, sides)

    grad_rows = 4 * hidden + hidden + channels
    part = grad_rows // n
    d_pair, total = pl.pallas_call(
        functools.partial(last_kernel, n, chunks, group, 1.0 / crop),
        name="pair_gradient",
        out_shape=(
            jax.ShapeDtypeStruct((steps, width, channels), BF16),
            jax.ShapeDtypeStruct((n, part, channels), F32),
        ),
        in_specs=[ANY] + [VMEM] * 8,
        out_specs=(VMEM, VMEM),
        scratch_shapes=[
            pltpu.VMEM(lr_shape, BF16),
            pltpu.VMEM((grad_rows, channels), F32),
            pltpu.VMEM((n, part, channels), F32),
            DMA((chunks, n)),
            DMA((chunks, n)),
            DMA((n,)),
            DMA((n,)),
            DMA((n,)),
            DMA((n,)),
            DMA,
        ],
        compiler_params=params(2),
    )(dlr, pair_q, normed, dgp, pmask, w_perm_t, w_perm, w_gate, grads)

    total = total.reshape((grad_rows, channels))
    total_in = total[: 4 * hidden].reshape((2, n, 2, hd, channels)).transpose((4, 2, 0, 1, 3))
    total_in = total_in.reshape((channels, 4 * hidden))
    return (
        update.reshape(pair.shape),
        d_pair.reshape(pair.shape),
        total_in,
        total[5 * hidden :],
        total[4 * hidden : 5 * hidden],
    )


def solution(mesh):
    in_specs = (
        P(("groups", "dap"), None, None),
        P(("groups", "dap"), None, None),
        P("groups"),
        P(),
        P(),
        P(),
    )
    out_specs = (
        P(("groups", "dap"), None, None),
        P(("groups", "dap"), None, None),
        P("groups", None),
        P("groups", None),
        P("groups", None),
    )
    body = functools.partial(shards, mesh.shape[AXIS])
    return jax.shard_map(body, mesh=mesh, in_specs=in_specs, out_specs=out_specs, check_vma=False)
```

```python
import functools
import math

import jax
import jax.numpy as jnp
from jax import lax
from jax.experimental import pallas as pl
from jax.experimental.pallas import tpu as pltpu
from jax.sharding import PartitionSpec as P

F32 = jnp.float32
BF16 = jnp.bfloat16
EPS = 1e-05
AXIS = "dap"
LANES = 128


def greet(n):
    me = lax.axis_index(AXIS)
    barrier = pltpu.get_barrier_semaphore()

    def one(step, carry):
        peer = lax.rem(me + step, n)
        pl.semaphore_signal(barrier, inc=1, device_id={AXIS: peer}, device_id_type=pl.DeviceIdType.MESH)
        return carry

    lax.fori_loop(1, n, one, 0)
    pl.semaphore_wait(barrier, n - 1)


def push(src, dst, send_sem, recv_sem, peer):
    return pltpu.make_async_remote_copy(
        src_ref=src,
        dst_ref=dst,
        send_sem=send_sem,
        recv_sem=recv_sem,
        device_id={AXIS: peer},
        device_id_type=pl.DeviceIdType.MESH,
    )


def push_chunk(n, c, src, dst, send_sem, recv_sem):
    me = lax.axis_index(AXIS)

    def one(step, carry):
        peer = lax.rem(me + step, n)
        push(src.at[peer, c], dst.at[me, c], send_sem.at[c, peer], recv_sem.at[c, me], peer).start()
        return carry

    lax.fori_loop(1, n, one, 0)


def await_recv(n, c, src, dst, send_sem, recv_sem):
    me = lax.axis_index(AXIS)

    def one(step, carry):
        peer = lax.rem(me + n - step, n)
        push(src.at[peer, c], dst.at[peer, c], send_sem.at[c, peer], recv_sem.at[c, peer], peer).wait_recv()
        return carry

    lax.fori_loop(1, n, one, 0)


def await_send(n, c, src, dst, send_sem, recv_sem):
    me = lax.axis_index(AXIS)

    def one(step, carry):
        peer = lax.rem(me + step, n)
        push(src.at[peer, c], dst.at[me, c], send_sem.at[c, peer], recv_sem.at[c, me], peer).wait_send()
        return carry

    lax.fori_loop(1, n, one, 0)


def dot(a, b, da, db):
    return lax.dot_general(a, b, (((da,), (db,)), ((), ())), preferred_element_type=F32)


def loop(count, body):
    def step(c, carry):
        body(c)
        return carry

    lax.fori_loop(0, count, step, 0)


def first_kernel(n, chunks, group, pair_ref, mask_ref, w_ref, normed_ref, out_ref, send, send_sem, recv_sem, own_sem):
    me = lax.axis_index(AXIS)
    greet(n)
    half = w_ref.shape[0] // 2
    rows = half // n
    width = pair_ref.shape[1]

    def body(c):
        for j in range(group):
            q = c * group + j
            x = pair_ref[q].astype(F32)
            center = x - jnp.mean(x, axis=-1, keepdims=True)
            inverse = lax.rsqrt(jnp.mean(center * center, axis=-1, keepdims=True) + EPS)
            normed = (center * inverse).astype(BF16)
            normed_ref[q] = normed
            lin = dot(w_ref[0:half, :], normed, 1, 1)
            gate = dot(w_ref[half:, :], normed, 1, 1)
            gated = (mask_ref[q] * jax.nn.sigmoid(gate) * lin).reshape((n, rows, width))
            send[:, c, j * rows : (j + 1) * rows, :] = gated.astype(BF16)
        push_chunk(n, c, send, out_ref, send_sem, recv_sem)

    loop(chunks, body)
    own = pltpu.make_async_copy(send.at[me], out_ref.at[me], own_sem)
    own.start()
    loop(chunks, lambda c: await_send(n, c, send, out_ref, send_sem, recv_sem))
    loop(chunks, lambda c: await_recv(n, c, send, out_ref, send_sem, recv_sem))
    own.wait()


def middle_kernel(
    n, chunks, group,
    tri_ref, normed_ref, cotan_ref, w_gate_ref, w_out_ref,
    update_ref, dgp_ref, grad_ref, out_ref,
    recv, send, in_send_sem, in_recv_sem, send_sem, recv_sem, own_sem,
):
    me = lax.axis_index(AXIS)
    greet(n)
    loop(chunks, lambda c: push_chunk(n, c, tri_ref, recv, in_send_sem, in_recv_sem))
    own_in = pltpu.make_async_copy(tri_ref.at[me], recv.at[me], own_sem.at[0])
    own_in.start()
    hidden = w_out_ref.shape[0]
    rows = hidden // n
    width = normed_ref.shape[1]
    grad_ref[...] = jnp.zeros_like(grad_ref)
    own_in.wait()

    def body(c):
        await_recv(n, c, tri_ref, recv, in_send_sem, in_recv_sem)
        block = recv[:, c].astype(F32)
        parts = []
        for j in range(group):
            q = c * group + j
            tri = block[:, j * rows : (j + 1) * rows, :].reshape((hidden, width))
            center = tri - jnp.mean(tri, axis=0, keepdims=True)
            inverse = lax.rsqrt(jnp.mean(center * center, axis=0, keepdims=True) + EPS)
            hat = center * inverse
            tri_normed = hat.astype(BF16)
            value = dot(tri_normed, w_out_ref[...], 0, 0)
            normed = normed_ref[q]
            out_gate = jax.nn.sigmoid(dot(normed, w_gate_ref[...], 1, 0))
            cotan = cotan_ref[q].astype(F32)
            update_ref[q] = (out_gate * value).astype(BF16)
            d_value = (cotan * out_gate).astype(BF16)
            dgp = (cotan * value * out_gate * (1.0 - out_gate)).astype(BF16)
            dgp_ref[q] = dgp
            grad_ref[0:hidden, :] += dot(tri_normed, d_value, 1, 0)
            grad_ref[hidden:, :] += dot(normed, dgp, 0, 0)
            d_tn = dot(w_out_ref[...], d_value, 1, 1)
            shifted = d_tn - jnp.mean(d_tn, axis=0, keepdims=True)
            d_tri = inverse * (shifted - hat * jnp.mean(d_tn * hat, axis=0, keepdims=True))
            parts.append(d_tri.reshape((n, rows, width)))
        send[:, c] = jnp.concatenate(parts, axis=1).astype(BF16)
        push_chunk(n, c, send, out_ref, send_sem, recv_sem)

    loop(chunks, body)
    own = pltpu.make_async_copy(send.at[me], out_ref.at[me], own_sem.at[1])
    own.start()
    loop(chunks, lambda c: await_send(n, c, tri_ref, recv, in_send_sem, in_recv_sem))
    loop(chunks, lambda c: await_send(n, c, send, out_ref, send_sem, recv_sem))
    loop(chunks, lambda c: await_recv(n, c, send, out_ref, send_sem, recv_sem))
    own.wait()


def last_kernel(
    n, chunks, group, scale,
    dlr_ref, pair_ref, normed_ref, dgp_ref, mask_ref, w_t_ref, w_ref, w_gate_ref, grad_ref,
    d_pair_ref, total_ref,
    recv, grads, slices, in_send_sem, in_recv_sem, rs_send, rs_recv, ag_send, ag_recv, own_sem,
):
    me = lax.axis_index(AXIS)
    greet(n)
    loop(chunks, lambda c: push_chunk(n, c, dlr_ref, recv, in_send_sem, in_recv_sem))
    own_in = pltpu.make_async_copy(dlr_ref.at[me], recv.at[me], own_sem)
    own_in.start()
    full = w_t_ref.shape[0]
    half = full // 2
    rows = half // n
    width = pair_ref.shape[1]
    part = slices.shape[1]
    channels = w_ref.shape[0]
    own_in.wait()

    def body(c):
        await_recv(n, c, dlr_ref, recv, in_send_sem, in_recv_sem)
        block = recv[:, c].astype(F32)
        for j in range(group):
            q = c * group + j
            cotan = block[:, j * rows : (j + 1) * rows, :].reshape((half, width)) * mask_ref[q]
            normed = normed_ref[q]
            lin = dot(w_t_ref[0:half, :], normed, 1, 1)
            sig = jax.nn.sigmoid(dot(w_t_ref[half:, :], normed, 1, 1))
            d_lin = cotan * sig
            d_gate = (d_lin * lin * (1.0 - sig)).astype(BF16)
            d_lin = d_lin.astype(BF16)
            grads[0:half, :] += dot(d_lin, normed, 1, 0)
            grads[half:full, :] += dot(d_gate, normed, 1, 0)
            d_normed = dot(w_ref[:, 0:half], d_lin, 1, 0) + dot(w_ref[:, half:], d_gate, 1, 0)
            d_normed = d_normed.T + dot(dgp_ref[q], w_gate_ref[...], 1, 1)
            x = pair_ref[q].astype(F32)
            center = x - jnp.mean(x, axis=-1, keepdims=True)
            inverse = lax.rsqrt(jnp.mean(center * center, axis=-1, keepdims=True) + EPS)
            hat = center * inverse
            shifted = d_normed - jnp.mean(d_normed, axis=-1, keepdims=True)
            d_pair = inverse * (shifted - hat * jnp.mean(d_normed * hat, axis=-1, keepdims=True))
            d_pair_ref[q] = d_pair.astype(BF16)

    grads[0:full, :] = jnp.zeros((full, channels), F32)
    grads[full:, :] = grad_ref[...]
    loop(chunks, body)

    def own_rows(d):
        return grads.at[pl.ds(pl.multiple_of(d * part, 8), part), :]

    def scatter(step, carry):
        peer = lax.rem(me + step, n)
        push(own_rows(peer), slices.at[me], rs_send.at[peer], rs_recv.at[me], peer).start()
        return carry

    lax.fori_loop(1, n, scatter, 0)
    slices[me] = grads[pl.ds(pl.multiple_of(me * part, 8), part), :]

    def scattered(step, carry):
        peer = lax.rem(me + n - step, n)
        push(own_rows(peer), slices.at[peer], rs_send.at[peer], rs_recv.at[peer], peer).wait_recv()
        return carry

    lax.fori_loop(1, n, scattered, 0)
    total = slices[0]
    for d in range(1, n):
        total = total + slices[d]
    total_ref[me] = total * scale

    def gather(step, carry):
        peer = lax.rem(me + step, n)
        push(total_ref.at[me], total_ref.at[me], ag_send.at[peer], ag_recv.at[me], peer).start()
        return carry

    lax.fori_loop(1, n, gather, 0)

    def gathered(step, carry):
        peer = lax.rem(me + n - step, n)
        push(total_ref.at[me], total_ref.at[peer], ag_send.at[peer], ag_recv.at[peer], peer).wait_recv()
        return carry

    lax.fori_loop(1, n, gathered, 0)

    def sent(step, carry):
        peer = lax.rem(me + step, n)
        push(own_rows(peer), slices.at[me], rs_send.at[peer], rs_recv.at[me], peer).wait_send()
        push(total_ref.at[me], total_ref.at[me], ag_send.at[peer], ag_recv.at[me], peer).wait_send()
        return carry

    lax.fori_loop(1, n, sent, 0)
    loop(chunks, lambda c: await_send(n, c, dlr_ref, recv, in_send_sem, in_recv_sem))


def take(ref, start, count, stride):
    return jnp.concatenate([ref[t, pl.ds(start, count, stride=stride), :] for t in range(ref.shape[0])], axis=1)


def put(ref, start, count, stride, values):
    short = ref.shape[0] * LANES - values.shape[1]
    if short:
        values = jnp.concatenate([values, jnp.zeros((values.shape[0], short), values.dtype)], axis=1)
    for t in range(ref.shape[0]):
        ref[t, pl.ds(start, count, stride=stride), :] = values[:, t * LANES : (t + 1) * LANES]


def unfold(wide, start, stride, fold):
    block = take(wide, start, wide.shape[1] // stride, stride).astype(BF16)
    crop = block.shape[1] // fold
    return jnp.concatenate([block[:, f * crop : (f + 1) * crop] for f in range(fold)], axis=0)


def refold(values, fold):
    count = values.shape[0] // fold
    return jnp.concatenate([values[f * count : (f + 1) * count, :] for f in range(fold)], axis=1)


def widen(n, src, wide):
    size = src.shape[1] * src.shape[2]

    def one(d):
        block = src[d].astype(F32).reshape((size, src.shape[3]))
        for t in range(wide.shape[0]):
            wide[t, pl.ds(pl.multiple_of(d * size, 8), size), :] = block[:, t * LANES : (t + 1) * LANES]

    loop(n, one)


def narrow(n, wide, dst):
    size = dst.shape[1] * dst.shape[2]

    def one(d):
        parts = [wide[t, pl.ds(pl.multiple_of(d * size, 8), size), :] for t in range(wide.shape[0])]
        dst[d] = jnp.concatenate(parts, axis=1).reshape(dst.shape[1:]).astype(BF16)

    loop(n, one)


def triangle_kernel(n, hd, fold, lr_ref, tri_ref, sides_ref, wide, rows, wire):
    widen(n, lr_ref, wide)
    count = wire.shape[1] // hd
    crop = sides_ref.shape[3]
    for h in range(hd):
        left = unfold(wide, h, 2 * hd, fold)
        right = unfold(wide, hd + h, 2 * hd, fold)
        sides_ref[0, h] = left
        sides_ref[1, h] = right
        put(rows, 0, count * fold, 1, dot(left, right, 0, 0))
        parts = [take(rows, f, count, fold)[:, :crop] for f in range(fold)]
        put(wire, h, count, hd, jnp.concatenate(parts, axis=1))
    narrow(n, wire, tri_ref)


def triangle_back_kernel(n, hd, fold, d_tri_ref, sides_ref, dlr_ref, wide, rows, wire):
    widen(n, d_tri_ref, wire)
    count = wire.shape[1] // hd
    crop = sides_ref.shape[3]
    for h in range(hd):
        block = take(wire, h, count, hd)
        for f in range(fold):
            put(rows, f, count, fold, block[:, f * crop : (f + 1) * crop])
        d_tri = take(rows, 0, count * fold, 1)[:, :crop].astype(BF16)
        d_left = dot(sides_ref[1, h], d_tri, 1, 1)
        d_right = dot(sides_ref[0, h], d_tri, 1, 0)
        put(wide, h, count, 2 * hd, refold(d_left, fold))
        put(wide, hd + h, count, 2 * hd, refold(d_right, fold))
    narrow(n, wide, dlr_ref)


def fused_kernel(
    n, hd, fold, chunks, group, chunks3, group3, scale,
    pair_ref, cotan_ref, mask_ref, w_t_ref, w_ref, w_gate_ref, w_out_ref,
    update_ref, d_pair_ref, total_ref,
    lr_send, lr_recv, dlr_send, dlr_recv, tri_send, tri_recv, dt_send, dt_recv,
    wide, rows_f, wire, sides, normed_s, dgp_s, grads, d_proj, sums, slices, gathered,
    lr_ss, lr_rs, dlr_ss, dlr_rs, tri_ss, tri_rs, dt_ss, dt_rs, rs_send, rs_recv, ag_send, ag_recv,
):
    me = lax.axis_index(AXIS)
    greet(n)
    full, channels = w_t_ref.shape
    half = full // 2
    hidden = w_out_ref.shape[0]
    lr_rows = 2 * hd
    width = pair_ref.shape[1]
    crop = sides.shape[3]
    part = sums.shape[0] // n

    def spread(block, dst, row, size):
        values = block.astype(F32)
        for t in range(dst.shape[0]):
            dst[t, pl.ds(pl.multiple_of(row, 8), size), :] = values[:, t * LANES : (t + 1) * LANES]

    def collect(c, count, src, dst, own, ss, rs, wide_ref):
        size = src.shape[2]
        spread(own[me, c], wide_ref, (me * count + c) * size, size)

        def one(step, carry):
            peer = lax.rem(me + n - step, n)
            push(src.at[peer, c], dst.at[peer, c], ss.at[c, peer], rs.at[c, peer], peer).wait_recv()
            spread(dst[peer, c], wide_ref, (peer * count + c) * size, size)
            return carry

        lax.fori_loop(1, n, one, 0)

    def distribute(c, count, wide_ref, src, dst, ss, rs):
        size = src.shape[2]

        def one(d):
            row = pl.multiple_of((d * count + c) * size, 8)
            parts = [wide_ref[t, pl.ds(row, size), :] for t in range(wide_ref.shape[0])]
            src[d, c] = jnp.concatenate(parts, axis=1).astype(BF16)

        loop(n, one)
        dst[me, c] = src[me, c]
        push_chunk(n, c, src, dst, ss, rs)

    def project(c):
        for j in range(group):
            q = c * group + j
            x = pair_ref[q].astype(F32)
            center = x - jnp.mean(x, axis=-1, keepdims=True)
            inverse = lax.rsqrt(jnp.mean(center * center, axis=-1, keepdims=True) + EPS)
            normed = (center * inverse).astype(BF16)
            normed_s[q] = normed
            lin = dot(w_t_ref[0:half, :], normed, 1, 1)
            gate = dot(w_t_ref[half:, :], normed, 1, 1)
            gated = (mask_ref[q] * jax.nn.sigmoid(gate) * lin).reshape((n, lr_rows, width))
            lr_send[:, c, j * lr_rows : (j + 1) * lr_rows, :] = gated.astype(BF16)
        push_chunk(n, c, lr_send, lr_recv, lr_ss, lr_rs)

    loop(chunks, project)
    grads[...] = jnp.zeros_like(grads)
    loop(chunks, lambda c: collect(c, chunks, lr_send, lr_recv, lr_send, lr_ss, lr_rs, wide))

    count = wire.shape[1] // hd
    for h in range(hd):
        left = unfold(wide, h, lr_rows, fold)
        right = unfold(wide, hd + h, lr_rows, fold)
        sides[0, h] = left
        sides[1, h] = right
        put(rows_f, 0, count * fold, 1, dot(left, right, 0, 0))
        parts = [take(rows_f, f, count, fold)[:, :crop] for f in range(fold)]
        put(wire, h, count, hd, jnp.concatenate(parts, axis=1))
    loop(chunks3, lambda c: distribute(c, chunks3, wire, tri_send, tri_recv, tri_ss, tri_rs))

    def middle(c):
        await_recv(n, c, tri_send, tri_recv, tri_ss, tri_rs)
        block = tri_recv[:, c].astype(F32)
        parts = []
        for j in range(group3):
            q = c * group3 + j
            tri = block[:, j * hd : (j + 1) * hd, :].reshape((hidden, width))
            center = tri - jnp.mean(tri, axis=0, keepdims=True)
            inverse = lax.rsqrt(jnp.mean(center * center, axis=0, keepdims=True) + EPS)
            hat = center * inverse
            tri_normed = hat.astype(BF16)
            value = dot(tri_normed, w_out_ref[...], 0, 0)
            normed = normed_s[q]
            out_gate = jax.nn.sigmoid(dot(normed, w_gate_ref[...], 1, 0))
            cotan = cotan_ref[q].astype(F32)
            update_ref[q] = (out_gate * value).astype(BF16)
            d_value = (cotan * out_gate).astype(BF16)
            dgp = (cotan * value * out_gate * (1.0 - out_gate)).astype(BF16)
            dgp_s[q] = dgp
            grads[full : full + hidden, :] += dot(tri_normed, d_value, 1, 0)
            grads[full + hidden :, :] += dot(normed, dgp, 0, 0)
            d_tn = dot(w_out_ref[...], d_value, 1, 1)
            shifted = d_tn - jnp.mean(d_tn, axis=0, keepdims=True)
            d_tri = inverse * (shifted - hat * jnp.mean(d_tn * hat, axis=0, keepdims=True))
            parts.append(d_tri.reshape((n, hd, width)))
        dt_send[:, c] = jnp.concatenate(parts, axis=1).astype(BF16)
        push_chunk(n, c, dt_send, dt_recv, dt_ss, dt_rs)

    loop(chunks3, middle)
    loop(chunks3, lambda c: collect(c, chunks3, dt_send, dt_recv, dt_send, dt_ss, dt_rs, wire))

    for h in range(hd):
        block = take(wire, h, count, hd)
        for f in range(fold):
            put(rows_f, f, count, fold, block[:, f * crop : (f + 1) * crop])
        d_tri = take(rows_f, 0, count * fold, 1)[:, :crop].astype(BF16)
        put(wide, h, count, lr_rows, refold(dot(sides[1, h], d_tri, 1, 1), fold))
        put(wide, hd + h, count, lr_rows, refold(dot(sides[0, h], d_tri, 1, 0), fold))
    loop(chunks, lambda c: distribute(c, chunks, wide, dlr_send, dlr_recv, dlr_ss, dlr_rs))

    def back_projection(c):
        await_recv(n, c, dlr_send, dlr_recv, dlr_ss, dlr_rs)
        block = dlr_recv[:, c].astype(F32)
        for j in range(group):
            q = c * group + j
            cotan = block[:, j * lr_rows : (j + 1) * lr_rows, :].reshape((half, width)) * mask_ref[q]
            normed = normed_s[q]
            lin = dot(w_t_ref[0:half, :], normed, 1, 1)
            sig = jax.nn.sigmoid(dot(w_t_ref[half:, :], normed, 1, 1))
            d_lin = cotan * sig
            d_gate = (d_lin * lin * (1.0 - sig)).astype(BF16)
            d_lin = d_lin.astype(BF16)
            grads[0:half, :] += dot(d_lin, normed, 1, 0)
            grads[half:full, :] += dot(d_gate, normed, 1, 0)
            d_proj[j, 0:half, :] = d_lin
            d_proj[j, half:, :] = d_gate

    def pair_gradient(c):
        for j in range(group):
            q = c * group + j
            d_normed = dot(w_ref[...], d_proj[j], 1, 0)
            d_normed = d_normed.T + dot(dgp_s[q], w_gate_ref[...], 1, 1)
            x = pair_ref[q].astype(F32)
            center = x - jnp.mean(x, axis=-1, keepdims=True)
            inverse = lax.rsqrt(jnp.mean(center * center, axis=-1, keepdims=True) + EPS)
            hat = center * inverse
            shifted = d_normed - jnp.mean(d_normed, axis=-1, keepdims=True)
            d_pair = inverse * (shifted - hat * jnp.mean(d_normed * hat, axis=-1, keepdims=True))
            d_pair_ref[q] = d_pair.astype(BF16)

    def both(c):
        back_projection(c)
        pair_gradient(c)

    loop(chunks - 1, both)
    back_projection(chunks - 1)
    sums[...] = grads[...].astype(BF16)

    def own_rows(d):
        return sums.at[pl.ds(pl.multiple_of(d * part, 16), part), :]

    def scatter(step, carry):
        peer = lax.rem(me + step, n)
        push(own_rows(peer), slices.at[me], rs_send.at[peer], rs_recv.at[me], peer).start()
        return carry

    lax.fori_loop(1, n, scatter, 0)
    slices[me] = sums[pl.ds(pl.multiple_of(me * part, 16), part), :]
    pair_gradient(chunks - 1)

    def scattered(step, carry):
        peer = lax.rem(me + n - step, n)
        push(own_rows(peer), slices.at[peer], rs_send.at[peer], rs_recv.at[peer], peer).wait_recv()
        return carry

    lax.fori_loop(1, n, scattered, 0)
    total = slices[0].astype(F32)
    for d in range(1, n):
        total = total + slices[d].astype(F32)
    gathered[me] = (total * scale).astype(BF16)

    def gather(step, carry):
        peer = lax.rem(me + step, n)
        push(gathered.at[me], gathered.at[me], ag_send.at[peer], ag_recv.at[me], peer).start()
        return carry

    lax.fori_loop(1, n, gather, 0)
    loop(chunks, lambda c: await_send(n, c, lr_send, lr_recv, lr_ss, lr_rs))
    loop(chunks3, lambda c: await_send(n, c, tri_send, tri_recv, tri_ss, tri_rs))
    loop(chunks3, lambda c: await_send(n, c, dt_send, dt_recv, dt_ss, dt_rs))
    loop(chunks, lambda c: await_send(n, c, dlr_send, dlr_recv, dlr_ss, dlr_rs))

    def arrived(step, carry):
        peer = lax.rem(me + n - step, n)
        push(gathered.at[me], gathered.at[peer], ag_send.at[peer], ag_recv.at[peer], peer).wait_recv()
        return carry

    lax.fori_loop(1, n, arrived, 0)

    def sent(step, carry):
        peer = lax.rem(me + step, n)
        push(own_rows(peer), slices.at[me], rs_send.at[peer], rs_recv.at[me], peer).wait_send()
        push(gathered.at[me], gathered.at[me], ag_send.at[peer], ag_recv.at[me], peer).wait_send()
        return carry

    lax.fori_loop(1, n, sent, 0)
    total_ref[...] = gathered[...].astype(F32)


VMEM = pl.BlockSpec(memory_space=pltpu.VMEM)
ANY = pl.BlockSpec(memory_space=pl.ANY)
DMA = pltpu.SemaphoreType.DMA


def params(which):
    return pltpu.CompilerParams(collective_id=which, has_side_effects=True, vmem_limit_bytes=50 * 1024 * 1024)


def shards(n, pair, d_out, residue_mask, w_in, w_gate, w_out):
    row_count, crop, channels = pair.shape
    hidden = w_out.shape[0]
    hd = hidden // n
    fold = 128 // math.gcd(128, crop)
    width = fold * crop
    steps = row_count // fold
    me = lax.axis_index(AXIS)
    mask_all = residue_mask.astype(F32)
    mask_rows = lax.dynamic_slice_in_dim(mask_all, me * row_count, row_count, 0)
    pmask = (mask_rows[:, None] * mask_all[None, :]).reshape((steps, 1, width))
    w_perm = w_in.reshape((channels, 2, 2, n, hd)).transpose((0, 2, 3, 1, 4)).reshape((channels, 4 * hidden))
    w_perm_t = w_perm.T
    pair_q = pair.reshape((steps, width, channels))
    cotan_q = d_out.reshape((steps, width, channels))

    group = 32 // (2 * hd)
    chunks = steps // group
    lr_shape = (n, chunks, group * 2 * hd, width)
    group3 = 16 // hd
    chunks3 = steps // group3
    tri_shape = (n, chunks3, group3 * hd, width)
    crop_rows = n * row_count
    relayout = [
        pltpu.VMEM((width // LANES, n * steps * 2 * hd, LANES), F32),
        pltpu.VMEM(((crop + LANES - 1) // LANES, crop_rows, LANES), F32),
        pltpu.VMEM((width // LANES, n * steps * hd, LANES), F32),
    ]
    grad_rows = 4 * hidden + hidden + channels
    part = grad_rows // n
    if part % 16 == 0 and 54 * pair.size < 48 * 1024 * 1024:
        buffers = [lr_shape] * 4 + [tri_shape] * 4
        rest = [
            pltpu.VMEM((2, hd, crop_rows, crop), BF16),
            pltpu.VMEM((steps, width, channels), BF16),
            pltpu.VMEM((steps, width, channels), BF16),
            pltpu.VMEM((grad_rows, channels), F32),
            pltpu.VMEM((group, 4 * hidden, width), BF16),
            pltpu.VMEM((grad_rows, channels), BF16),
            pltpu.VMEM((n, part, channels), BF16),
            pltpu.VMEM((n, part, channels), BF16),
        ]
        update, d_pair, total = pl.pallas_call(
            functools.partial(fused_kernel, n, hd, fold, chunks, group, chunks3, group3, 1.0 / crop),
            name="triangle_update",
            out_shape=(
                jax.ShapeDtypeStruct((steps, width, channels), BF16),
                jax.ShapeDtypeStruct((steps, width, channels), BF16),
                jax.ShapeDtypeStruct((n, part, channels), F32),
            ),
            in_specs=[VMEM] * 7,
            out_specs=(VMEM, VMEM, VMEM),
            scratch_shapes=[pltpu.VMEM(shape, BF16) for shape in buffers]
            + relayout
            + rest
            + [DMA((chunks, n))] * 4
            + [DMA((chunks3, n))] * 4
            + [DMA((n,))] * 4,
            compiler_params=pltpu.CompilerParams(
                collective_id=3, has_side_effects=True, vmem_limit_bytes=54 * 1024 * 1024
            ),
        )(pair_q, cotan_q, pmask, w_perm_t, w_perm, w_gate, w_out)
    else:
        normed, lr = pl.pallas_call(
            functools.partial(first_kernel, n, chunks, group),
            name="project_and_send",
            out_shape=(
                jax.ShapeDtypeStruct((steps, width, channels), BF16),
                jax.ShapeDtypeStruct(lr_shape, BF16),
            ),
            in_specs=[VMEM] * 3,
            out_specs=(VMEM, ANY),
            scratch_shapes=[pltpu.VMEM(lr_shape, BF16), DMA((chunks, n)), DMA((chunks, n)), DMA],
            compiler_params=params(0),
        )(pair_q, pmask, w_perm_t)

        tri, sides = pl.pallas_call(
            functools.partial(triangle_kernel, n, hd, fold),
            name="triangle",
            out_shape=(
                jax.ShapeDtypeStruct(tri_shape, BF16),
                jax.ShapeDtypeStruct((2, hd, crop_rows, crop), BF16),
            ),
            in_specs=[VMEM],
            out_specs=(VMEM, VMEM),
            scratch_shapes=relayout,
            compiler_params=pltpu.CompilerParams(vmem_limit_bytes=50 * 1024 * 1024),
        )(lr)

        update, dgp, grads, d_tri = pl.pallas_call(
            functools.partial(middle_kernel, n, chunks3, group3),
            name="gate_and_back",
            out_shape=(
                jax.ShapeDtypeStruct((steps, width, channels), BF16),
                jax.ShapeDtypeStruct((steps, width, channels), BF16),
                jax.ShapeDtypeStruct((hidden + channels, channels), F32),
                jax.ShapeDtypeStruct(tri_shape, BF16),
            ),
            in_specs=[ANY] + [VMEM] * 4,
            out_specs=(VMEM, VMEM, VMEM, ANY),
            scratch_shapes=[
                pltpu.VMEM(tri_shape, BF16),
                pltpu.VMEM(tri_shape, BF16),
                DMA((chunks3, n)),
                DMA((chunks3, n)),
                DMA((chunks3, n)),
                DMA((chunks3, n)),
                DMA((2,)),
            ],
            compiler_params=params(1),
        )(tri, normed, cotan_q, w_gate, w_out)

        dlr = pl.pallas_call(
            functools.partial(triangle_back_kernel, n, hd, fold),
            name="triangle_back",
            out_shape=jax.ShapeDtypeStruct(lr_shape, BF16),
            in_specs=[VMEM, VMEM],
            out_specs=VMEM,
            scratch_shapes=relayout,
            compiler_params=pltpu.CompilerParams(vmem_limit_bytes=50 * 1024 * 1024),
        )(d_tri, sides)

        d_pair, total = pl.pallas_call(
            functools.partial(last_kernel, n, chunks, group, 1.0 / crop),
            name="pair_gradient",
            out_shape=(
                jax.ShapeDtypeStruct((steps, width, channels), BF16),
                jax.ShapeDtypeStruct((n, part, channels), F32),
            ),
            in_specs=[ANY] + [VMEM] * 8,
            out_specs=(VMEM, VMEM),
            scratch_shapes=[
                pltpu.VMEM(lr_shape, BF16),
                pltpu.VMEM((grad_rows, channels), F32),
                pltpu.VMEM((n, part, channels), F32),
                DMA((chunks, n)),
                DMA((chunks, n)),
                DMA((n,)),
                DMA((n,)),
                DMA((n,)),
                DMA((n,)),
                DMA,
            ],
            compiler_params=params(2),
        )(dlr, pair_q, normed, dgp, pmask, w_perm_t, w_perm, w_gate, grads)

    total = total.reshape((grad_rows, channels))
    total_in = total[: 4 * hidden].reshape((2, n, 2, hd, channels)).transpose((4, 2, 0, 1, 3))
    total_in = total_in.reshape((channels, 4 * hidden))
    return (
        update.reshape(pair.shape),
        d_pair.reshape(pair.shape),
        total_in,
        total[5 * hidden :],
        total[4 * hidden : 5 * hidden],
    )


def solution(mesh):
    in_specs = (
        P(("groups", "dap"), None, None),
        P(("groups", "dap"), None, None),
        P("groups"),
        P(),
        P(),
        P(),
    )
    out_specs = (
        P(("groups", "dap"), None, None),
        P(("groups", "dap"), None, None),
        P("groups", None),
        P("groups", None),
        P("groups", None),
    )
    body = functools.partial(shards, mesh.shape[AXIS])
    return jax.shard_map(body, mesh=mesh, in_specs=in_specs, out_specs=out_specs, check_vma=False)
```

```python
import functools
import math

import jax
import jax.numpy as jnp
from jax import lax
from jax.experimental import pallas as pl
from jax.experimental.pallas import tpu as pltpu
from jax.sharding import PartitionSpec as P

F32 = jnp.float32
BF16 = jnp.bfloat16
EPS = 1e-05
AXIS = "dap"
LANES = 128


def greet(n):
    me = lax.axis_index(AXIS)
    barrier = pltpu.get_barrier_semaphore()

    def one(step, carry):
        peer = lax.rem(me + step, n)
        pl.semaphore_signal(barrier, inc=1, device_id={AXIS: peer}, device_id_type=pl.DeviceIdType.MESH)
        return carry

    lax.fori_loop(1, n, one, 0)
    pl.semaphore_wait(barrier, n - 1)


def push(src, dst, send_sem, recv_sem, peer):
    return pltpu.make_async_remote_copy(
        src_ref=src,
        dst_ref=dst,
        send_sem=send_sem,
        recv_sem=recv_sem,
        device_id={AXIS: peer},
        device_id_type=pl.DeviceIdType.MESH,
    )


def push_chunk(n, c, src, dst, send_sem, recv_sem):
    me = lax.axis_index(AXIS)

    def one(step, carry):
        peer = lax.rem(me + step, n)
        push(src.at[peer, c], dst.at[me, c], send_sem.at[c, peer], recv_sem.at[c, me], peer).start()
        return carry

    lax.fori_loop(1, n, one, 0)


def await_recv(n, c, src, dst, send_sem, recv_sem):
    me = lax.axis_index(AXIS)

    def one(step, carry):
        peer = lax.rem(me + n - step, n)
        push(src.at[peer, c], dst.at[peer, c], send_sem.at[c, peer], recv_sem.at[c, peer], peer).wait_recv()
        return carry

    lax.fori_loop(1, n, one, 0)


def await_send(n, c, src, dst, send_sem, recv_sem):
    me = lax.axis_index(AXIS)

    def one(step, carry):
        peer = lax.rem(me + step, n)
        push(src.at[peer, c], dst.at[me, c], send_sem.at[c, peer], recv_sem.at[c, me], peer).wait_send()
        return carry

    lax.fori_loop(1, n, one, 0)


def dot(a, b, da, db):
    return lax.dot_general(a, b, (((da,), (db,)), ((), ())), preferred_element_type=F32)


def loop(count, body):
    def step(c, carry):
        body(c)
        return carry

    lax.fori_loop(0, count, step, 0)


def first_kernel(n, chunks, group, pair_ref, mask_ref, w_ref, normed_ref, out_ref, send, send_sem, recv_sem, own_sem):
    me = lax.axis_index(AXIS)
    greet(n)
    half = w_ref.shape[0] // 2
    rows = half // n
    width = pair_ref.shape[1]

    def body(c):
        for j in range(group):
            q = c * group + j
            x = pair_ref[q].astype(F32)
            center = x - jnp.mean(x, axis=-1, keepdims=True)
            inverse = lax.rsqrt(jnp.mean(center * center, axis=-1, keepdims=True) + EPS)
            normed = (center * inverse).astype(BF16)
            normed_ref[q] = normed
            lin = dot(w_ref[0:half, :], normed, 1, 1)
            gate = dot(w_ref[half:, :], normed, 1, 1)
            gated = (mask_ref[q] * jax.nn.sigmoid(gate) * lin).reshape((n, rows, width))
            send[:, c, j * rows : (j + 1) * rows, :] = gated.astype(BF16)
        push_chunk(n, c, send, out_ref, send_sem, recv_sem)

    loop(chunks, body)
    own = pltpu.make_async_copy(send.at[me], out_ref.at[me], own_sem)
    own.start()
    loop(chunks, lambda c: await_send(n, c, send, out_ref, send_sem, recv_sem))
    loop(chunks, lambda c: await_recv(n, c, send, out_ref, send_sem, recv_sem))
    own.wait()


def middle_kernel(
    n, chunks, group,
    tri_ref, normed_ref, cotan_ref, w_gate_ref, w_out_ref,
    update_ref, dgp_ref, grad_ref, out_ref,
    recv, send, in_send_sem, in_recv_sem, send_sem, recv_sem, own_sem,
):
    me = lax.axis_index(AXIS)
    greet(n)
    loop(chunks, lambda c: push_chunk(n, c, tri_ref, recv, in_send_sem, in_recv_sem))
    own_in = pltpu.make_async_copy(tri_ref.at[me], recv.at[me], own_sem.at[0])
    own_in.start()
    hidden = w_out_ref.shape[0]
    rows = hidden // n
    width = normed_ref.shape[1]
    grad_ref[...] = jnp.zeros_like(grad_ref)
    own_in.wait()

    def body(c):
        await_recv(n, c, tri_ref, recv, in_send_sem, in_recv_sem)
        block = recv[:, c].astype(F32)
        parts = []
        for j in range(group):
            q = c * group + j
            tri = block[:, j * rows : (j + 1) * rows, :].reshape((hidden, width))
            center = tri - jnp.mean(tri, axis=0, keepdims=True)
            inverse = lax.rsqrt(jnp.mean(center * center, axis=0, keepdims=True) + EPS)
            hat = center * inverse
            tri_normed = hat.astype(BF16)
            value = dot(tri_normed, w_out_ref[...], 0, 0)
            normed = normed_ref[q]
            out_gate = jax.nn.sigmoid(dot(normed, w_gate_ref[...], 1, 0))
            cotan = cotan_ref[q].astype(F32)
            update_ref[q] = (out_gate * value).astype(BF16)
            d_value = (cotan * out_gate).astype(BF16)
            dgp = (cotan * value * out_gate * (1.0 - out_gate)).astype(BF16)
            dgp_ref[q] = dgp
            grad_ref[0:hidden, :] += dot(tri_normed, d_value, 1, 0)
            grad_ref[hidden:, :] += dot(normed, dgp, 0, 0)
            d_tn = dot(w_out_ref[...], d_value, 1, 1)
            shifted = d_tn - jnp.mean(d_tn, axis=0, keepdims=True)
            d_tri = inverse * (shifted - hat * jnp.mean(d_tn * hat, axis=0, keepdims=True))
            parts.append(d_tri.reshape((n, rows, width)))
        send[:, c] = jnp.concatenate(parts, axis=1).astype(BF16)
        push_chunk(n, c, send, out_ref, send_sem, recv_sem)

    loop(chunks, body)
    own = pltpu.make_async_copy(send.at[me], out_ref.at[me], own_sem.at[1])
    own.start()
    loop(chunks, lambda c: await_send(n, c, tri_ref, recv, in_send_sem, in_recv_sem))
    loop(chunks, lambda c: await_send(n, c, send, out_ref, send_sem, recv_sem))
    loop(chunks, lambda c: await_recv(n, c, send, out_ref, send_sem, recv_sem))
    own.wait()


def last_kernel(
    n, chunks, group, scale,
    dlr_ref, pair_ref, normed_ref, dgp_ref, mask_ref, w_t_ref, w_ref, w_gate_ref, grad_ref,
    d_pair_ref, total_ref,
    recv, grads, slices, in_send_sem, in_recv_sem, rs_send, rs_recv, ag_send, ag_recv, own_sem,
):
    me = lax.axis_index(AXIS)
    greet(n)
    loop(chunks, lambda c: push_chunk(n, c, dlr_ref, recv, in_send_sem, in_recv_sem))
    own_in = pltpu.make_async_copy(dlr_ref.at[me], recv.at[me], own_sem)
    own_in.start()
    full = w_t_ref.shape[0]
    half = full // 2
    rows = half // n
    width = pair_ref.shape[1]
    part = slices.shape[1]
    channels = w_ref.shape[0]
    own_in.wait()

    def body(c):
        await_recv(n, c, dlr_ref, recv, in_send_sem, in_recv_sem)
        block = recv[:, c].astype(F32)
        for j in range(group):
            q = c * group + j
            cotan = block[:, j * rows : (j + 1) * rows, :].reshape((half, width)) * mask_ref[q]
            normed = normed_ref[q]
            lin = dot(w_t_ref[0:half, :], normed, 1, 1)
            sig = jax.nn.sigmoid(dot(w_t_ref[half:, :], normed, 1, 1))
            d_lin = cotan * sig
            d_gate = (d_lin * lin * (1.0 - sig)).astype(BF16)
            d_lin = d_lin.astype(BF16)
            grads[0:half, :] += dot(d_lin, normed, 1, 0)
            grads[half:full, :] += dot(d_gate, normed, 1, 0)
            d_normed = dot(w_ref[:, 0:half], d_lin, 1, 0) + dot(w_ref[:, half:], d_gate, 1, 0)
            d_normed = d_normed.T + dot(dgp_ref[q], w_gate_ref[...], 1, 1)
            x = pair_ref[q].astype(F32)
            center = x - jnp.mean(x, axis=-1, keepdims=True)
            inverse = lax.rsqrt(jnp.mean(center * center, axis=-1, keepdims=True) + EPS)
            hat = center * inverse
            shifted = d_normed - jnp.mean(d_normed, axis=-1, keepdims=True)
            d_pair = inverse * (shifted - hat * jnp.mean(d_normed * hat, axis=-1, keepdims=True))
            d_pair_ref[q] = d_pair.astype(BF16)

    grads[0:full, :] = jnp.zeros((full, channels), F32)
    grads[full:, :] = grad_ref[...]
    loop(chunks, body)

    def own_rows(d):
        return grads.at[pl.ds(pl.multiple_of(d * part, 8), part), :]

    def scatter(step, carry):
        peer = lax.rem(me + step, n)
        push(own_rows(peer), slices.at[me], rs_send.at[peer], rs_recv.at[me], peer).start()
        return carry

    lax.fori_loop(1, n, scatter, 0)
    slices[me] = grads[pl.ds(pl.multiple_of(me * part, 8), part), :]

    def scattered(step, carry):
        peer = lax.rem(me + n - step, n)
        push(own_rows(peer), slices.at[peer], rs_send.at[peer], rs_recv.at[peer], peer).wait_recv()
        return carry

    lax.fori_loop(1, n, scattered, 0)
    total = slices[0]
    for d in range(1, n):
        total = total + slices[d]
    total_ref[me] = total * scale

    def gather(step, carry):
        peer = lax.rem(me + step, n)
        push(total_ref.at[me], total_ref.at[me], ag_send.at[peer], ag_recv.at[me], peer).start()
        return carry

    lax.fori_loop(1, n, gather, 0)

    def gathered(step, carry):
        peer = lax.rem(me + n - step, n)
        push(total_ref.at[me], total_ref.at[peer], ag_send.at[peer], ag_recv.at[peer], peer).wait_recv()
        return carry

    lax.fori_loop(1, n, gathered, 0)

    def sent(step, carry):
        peer = lax.rem(me + step, n)
        push(own_rows(peer), slices.at[me], rs_send.at[peer], rs_recv.at[me], peer).wait_send()
        push(total_ref.at[me], total_ref.at[me], ag_send.at[peer], ag_recv.at[me], peer).wait_send()
        return carry

    lax.fori_loop(1, n, sent, 0)
    loop(chunks, lambda c: await_send(n, c, dlr_ref, recv, in_send_sem, in_recv_sem))


def take(ref, start, count, stride):
    return jnp.concatenate([ref[t, pl.ds(start, count, stride=stride), :] for t in range(ref.shape[0])], axis=1)


def put(ref, start, count, stride, values):
    short = ref.shape[0] * LANES - values.shape[1]
    if short:
        values = jnp.concatenate([values, jnp.zeros((values.shape[0], short), values.dtype)], axis=1)
    for t in range(ref.shape[0]):
        ref[t, pl.ds(start, count, stride=stride), :] = values[:, t * LANES : (t + 1) * LANES]


def unfold(wide, start, stride, fold):
    block = take(wide, start, wide.shape[1] // stride, stride).astype(BF16)
    crop = block.shape[1] // fold
    return jnp.concatenate([block[:, f * crop : (f + 1) * crop] for f in range(fold)], axis=0)


def refold(values, fold):
    count = values.shape[0] // fold
    return jnp.concatenate([values[f * count : (f + 1) * count, :] for f in range(fold)], axis=1)


def widen(n, src, wide):
    size = src.shape[1] * src.shape[2]

    def one(d):
        block = src[d].astype(F32).reshape((size, src.shape[3]))
        for t in range(wide.shape[0]):
            wide[t, pl.ds(pl.multiple_of(d * size, 8), size), :] = block[:, t * LANES : (t + 1) * LANES]

    loop(n, one)


def narrow(n, wide, dst):
    size = dst.shape[1] * dst.shape[2]

    def one(d):
        parts = [wide[t, pl.ds(pl.multiple_of(d * size, 8), size), :] for t in range(wide.shape[0])]
        dst[d] = jnp.concatenate(parts, axis=1).reshape(dst.shape[1:]).astype(BF16)

    loop(n, one)


def triangle_kernel(n, hd, fold, lr_ref, tri_ref, sides_ref, wide, rows, wire):
    widen(n, lr_ref, wide)
    count = wire.shape[1] // hd
    crop = sides_ref.shape[3]
    for h in range(hd):
        left = unfold(wide, h, 2 * hd, fold)
        right = unfold(wide, hd + h, 2 * hd, fold)
        sides_ref[0, h] = left
        sides_ref[1, h] = right
        put(rows, 0, count * fold, 1, dot(left, right, 0, 0))
        parts = [take(rows, f, count, fold)[:, :crop] for f in range(fold)]
        put(wire, h, count, hd, jnp.concatenate(parts, axis=1))
    narrow(n, wire, tri_ref)


def triangle_back_kernel(n, hd, fold, d_tri_ref, sides_ref, dlr_ref, wide, rows, wire):
    widen(n, d_tri_ref, wire)
    count = wire.shape[1] // hd
    crop = sides_ref.shape[3]
    for h in range(hd):
        block = take(wire, h, count, hd)
        for f in range(fold):
            put(rows, f, count, fold, block[:, f * crop : (f + 1) * crop])
        d_tri = take(rows, 0, count * fold, 1)[:, :crop].astype(BF16)
        d_left = dot(sides_ref[1, h], d_tri, 1, 1)
        d_right = dot(sides_ref[0, h], d_tri, 1, 0)
        put(wide, h, count, 2 * hd, refold(d_left, fold))
        put(wide, hd + h, count, 2 * hd, refold(d_right, fold))
    narrow(n, wide, dlr_ref)


def fused_kernel(
    n, hd, fold, splits, chunks, group, chunks3, group3, scale,
    pair_ref, cotan_ref, mask_ref, w_t_ref, w_ref, w_gate_ref, w_out_ref,
    update_ref, d_pair_ref, total_ref,
    lr_send, lr_recv, dlr_send, dlr_recv, tri_send, tri_recv, dt_send, dt_recv,
    wide, rows_f, wire, sides, normed_s, dgp_s, grads, d_proj, sums, slices, gathered,
    lr_ss, lr_rs, dlr_ss, dlr_rs, tri_ss, tri_rs, dt_ss, dt_rs, rs_send, rs_recv, ag_send, ag_recv,
):
    me = lax.axis_index(AXIS)
    greet(n)
    full, channels = w_t_ref.shape
    half = full // 2
    hidden = w_out_ref.shape[0]
    lr_rows = 2 * hd // splits
    span = hd // splits
    width = pair_ref.shape[1]
    crop = sides.shape[3]
    part = sums.shape[0] // n

    def spread(block, dst, row, size):
        values = block.astype(F32)
        for t in range(dst.shape[0]):
            dst[t, pl.ds(pl.multiple_of(row, 8), size), :] = values[:, t * LANES : (t + 1) * LANES]

    def collect(c, s, count, src, dst, own, ss, rs, wide_ref):
        size = src.shape[2]
        base = s * n * count * size
        i = s * count + c
        spread(own[me, i], wide_ref, base + (me * count + c) * size, size)

        def one(step, carry):
            peer = lax.rem(me + n - step, n)
            push(src.at[peer, i], dst.at[peer, i], ss.at[i, peer], rs.at[i, peer], peer).wait_recv()
            spread(dst[peer, i], wide_ref, base + (peer * count + c) * size, size)
            return carry

        lax.fori_loop(1, n, one, 0)

    def distribute(c, s, count, wide_ref, src, dst, ss, rs):
        size = src.shape[2]
        base = s * n * count * size
        i = s * count + c

        def one(d):
            row = pl.multiple_of(base + (d * count + c) * size, 8)
            parts = [wide_ref[t, pl.ds(row, size), :] for t in range(wide_ref.shape[0])]
            src[d, i] = jnp.concatenate(parts, axis=1).astype(BF16)

        loop(n, one)
        dst[me, i] = src[me, i]
        push_chunk(n, i, src, dst, ss, rs)

    def project(c):
        for j in range(group):
            q = c * group + j
            x = pair_ref[q].astype(F32)
            center = x - jnp.mean(x, axis=-1, keepdims=True)
            inverse = lax.rsqrt(jnp.mean(center * center, axis=-1, keepdims=True) + EPS)
            normed = (center * inverse).astype(BF16)
            normed_s[q] = normed
            lin = dot(w_t_ref[0:half, :], normed, 1, 1)
            gate = dot(w_t_ref[half:, :], normed, 1, 1)
            gated = (mask_ref[q] * jax.nn.sigmoid(gate) * lin).reshape((n, splits, lr_rows, width))
            for s in range(splits):
                lr_send[:, s * chunks + c, j * lr_rows : (j + 1) * lr_rows, :] = gated[:, s].astype(BF16)
        push_chunk(n, c, lr_send, lr_recv, lr_ss, lr_rs)

    loop(chunks, project)
    for s in range(1, splits):
        loop(chunks, lambda c: push_chunk(n, s * chunks + c, lr_send, lr_recv, lr_ss, lr_rs))
    grads[...] = jnp.zeros_like(grads)

    count = wire.shape[1] // hd

    def side(s, t, k):
        block = take(wide, s * count * lr_rows + t * span + k, count, lr_rows).astype(BF16)
        return jnp.concatenate([block[:, f * crop : (f + 1) * crop] for f in range(fold)], axis=0)

    for s in range(splits):
        loop(chunks, lambda c: collect(c, s, chunks, lr_send, lr_recv, lr_send, lr_ss, lr_rs, wide))
        for k in range(span):
            h = s * span + k
            left = side(s, 0, k)
            right = side(s, 1, k)
            sides[0, h] = left
            sides[1, h] = right
            put(rows_f, 0, count * fold, 1, dot(left, right, 0, 0))
            parts = [take(rows_f, f, count, fold)[:, :crop] for f in range(fold)]
            put(wire, h, count, hd, jnp.concatenate(parts, axis=1))
    loop(chunks3, lambda c: distribute(c, 0, chunks3, wire, tri_send, tri_recv, tri_ss, tri_rs))

    def middle(c):
        await_recv(n, c, tri_send, tri_recv, tri_ss, tri_rs)
        block = tri_recv[:, c].astype(F32)
        parts = []
        for j in range(group3):
            q = c * group3 + j
            tri = block[:, j * hd : (j + 1) * hd, :].reshape((hidden, width))
            center = tri - jnp.mean(tri, axis=0, keepdims=True)
            inverse = lax.rsqrt(jnp.mean(center * center, axis=0, keepdims=True) + EPS)
            hat = center * inverse
            tri_normed = hat.astype(BF16)
            value = dot(tri_normed, w_out_ref[...], 0, 0)
            normed = normed_s[q]
            out_gate = jax.nn.sigmoid(dot(normed, w_gate_ref[...], 1, 0))
            cotan = cotan_ref[q].astype(F32)
            update_ref[q] = (out_gate * value).astype(BF16)
            d_value = (cotan * out_gate).astype(BF16)
            dgp = (cotan * value * out_gate * (1.0 - out_gate)).astype(BF16)
            dgp_s[q] = dgp
            grads[full : full + hidden, :] += dot(tri_normed, d_value, 1, 0)
            grads[full + hidden :, :] += dot(normed, dgp, 0, 0)
            d_tn = dot(w_out_ref[...], d_value, 1, 1)
            shifted = d_tn - jnp.mean(d_tn, axis=0, keepdims=True)
            d_tri = inverse * (shifted - hat * jnp.mean(d_tn * hat, axis=0, keepdims=True))
            parts.append(d_tri.reshape((n, hd, width)))
        dt_send[:, c] = jnp.concatenate(parts, axis=1).astype(BF16)
        push_chunk(n, c, dt_send, dt_recv, dt_ss, dt_rs)

    loop(chunks3, middle)
    loop(chunks3, lambda c: collect(c, 0, chunks3, dt_send, dt_recv, dt_send, dt_ss, dt_rs, wire))

    for s in range(splits):
        for k in range(span):
            h = s * span + k
            block = take(wire, h, count, hd)
            for f in range(fold):
                put(rows_f, f, count, fold, block[:, f * crop : (f + 1) * crop])
            d_tri = take(rows_f, 0, count * fold, 1)[:, :crop].astype(BF16)
            start = s * count * lr_rows + k
            put(wide, start, count, lr_rows, refold(dot(sides[1, h], d_tri, 1, 1), fold))
            put(wide, start + span, count, lr_rows, refold(dot(sides[0, h], d_tri, 1, 0), fold))
        loop(chunks, lambda c: distribute(c, s, chunks, wide, dlr_send, dlr_recv, dlr_ss, dlr_rs))

    def back_projection(c):
        blocks = []
        for s in range(splits):
            await_recv(n, s * chunks + c, dlr_send, dlr_recv, dlr_ss, dlr_rs)
            blocks.append(dlr_recv[:, s * chunks + c].astype(F32))
        for j in range(group):
            q = c * group + j
            shares = [block[:, j * lr_rows : (j + 1) * lr_rows, :] for block in blocks]
            cotan = jnp.concatenate(shares, axis=1).reshape((half, width)) * mask_ref[q]
            normed = normed_s[q]
            lin = dot(w_t_ref[0:half, :], normed, 1, 1)
            sig = jax.nn.sigmoid(dot(w_t_ref[half:, :], normed, 1, 1))
            d_lin = cotan * sig
            d_gate = (d_lin * lin * (1.0 - sig)).astype(BF16)
            d_lin = d_lin.astype(BF16)
            grads[0:half, :] += dot(d_lin, normed, 1, 0)
            grads[half:full, :] += dot(d_gate, normed, 1, 0)
            d_proj[j, 0:half, :] = d_lin
            d_proj[j, half:, :] = d_gate

    def pair_gradient(c):
        for j in range(group):
            q = c * group + j
            d_normed = dot(w_ref[...], d_proj[j], 1, 0)
            d_normed = d_normed.T + dot(dgp_s[q], w_gate_ref[...], 1, 1)
            x = pair_ref[q].astype(F32)
            center = x - jnp.mean(x, axis=-1, keepdims=True)
            inverse = lax.rsqrt(jnp.mean(center * center, axis=-1, keepdims=True) + EPS)
            hat = center * inverse
            shifted = d_normed - jnp.mean(d_normed, axis=-1, keepdims=True)
            d_pair = inverse * (shifted - hat * jnp.mean(d_normed * hat, axis=-1, keepdims=True))
            d_pair_ref[q] = d_pair.astype(BF16)

    def both(c):
        back_projection(c)
        pair_gradient(c)

    loop(chunks - 1, both)
    back_projection(chunks - 1)
    sums[...] = grads[...].astype(BF16)

    def own_rows(d):
        return sums.at[pl.ds(pl.multiple_of(d * part, 16), part), :]

    def scatter(step, carry):
        peer = lax.rem(me + step, n)
        push(own_rows(peer), slices.at[me], rs_send.at[peer], rs_recv.at[me], peer).start()
        return carry

    lax.fori_loop(1, n, scatter, 0)
    slices[me] = sums[pl.ds(pl.multiple_of(me * part, 16), part), :]
    pair_gradient(chunks - 1)

    def scattered(step, carry):
        peer = lax.rem(me + n - step, n)
        push(own_rows(peer), slices.at[peer], rs_send.at[peer], rs_recv.at[peer], peer).wait_recv()
        return carry

    lax.fori_loop(1, n, scattered, 0)
    total = slices[0].astype(F32)
    for d in range(1, n):
        total = total + slices[d].astype(F32)
    gathered[me] = (total * scale).astype(BF16)

    def gather(step, carry):
        peer = lax.rem(me + step, n)
        push(gathered.at[me], gathered.at[me], ag_send.at[peer], ag_recv.at[me], peer).start()
        return carry

    lax.fori_loop(1, n, gather, 0)
    loop(splits * chunks, lambda c: await_send(n, c, lr_send, lr_recv, lr_ss, lr_rs))
    loop(chunks3, lambda c: await_send(n, c, tri_send, tri_recv, tri_ss, tri_rs))
    loop(chunks3, lambda c: await_send(n, c, dt_send, dt_recv, dt_ss, dt_rs))
    loop(splits * chunks, lambda c: await_send(n, c, dlr_send, dlr_recv, dlr_ss, dlr_rs))

    def arrived(step, carry):
        peer = lax.rem(me + n - step, n)
        push(gathered.at[me], gathered.at[peer], ag_send.at[peer], ag_recv.at[peer], peer).wait_recv()
        return carry

    lax.fori_loop(1, n, arrived, 0)

    def sent(step, carry):
        peer = lax.rem(me + step, n)
        push(own_rows(peer), slices.at[me], rs_send.at[peer], rs_recv.at[me], peer).wait_send()
        push(gathered.at[me], gathered.at[me], ag_send.at[peer], ag_recv.at[me], peer).wait_send()
        return carry

    lax.fori_loop(1, n, sent, 0)
    total_ref[...] = gathered[...].astype(F32)


VMEM = pl.BlockSpec(memory_space=pltpu.VMEM)
ANY = pl.BlockSpec(memory_space=pl.ANY)
DMA = pltpu.SemaphoreType.DMA


def params(which):
    return pltpu.CompilerParams(collective_id=which, has_side_effects=True, vmem_limit_bytes=50 * 1024 * 1024)


def shards(n, pair, d_out, residue_mask, w_in, w_gate, w_out):
    row_count, crop, channels = pair.shape
    hidden = w_out.shape[0]
    hd = hidden // n
    fold = 128 // math.gcd(128, crop)
    width = fold * crop
    steps = row_count // fold
    me = lax.axis_index(AXIS)
    mask_all = residue_mask.astype(F32)
    mask_rows = lax.dynamic_slice_in_dim(mask_all, me * row_count, row_count, 0)
    pmask = (mask_rows[:, None] * mask_all[None, :]).reshape((steps, 1, width))
    fused = 6 * hidden % (16 * n) == 0 and 54 * pair.size < 48 * 1024 * 1024
    splits = 2 if fused and hd % 8 == 0 else 1
    w_perm = w_in.reshape((channels, 2, 2, n, splits, hd // splits)).transpose((0, 2, 3, 4, 1, 5))
    w_perm = w_perm.reshape((channels, 4 * hidden))
    w_perm_t = w_perm.T
    pair_q = pair.reshape((steps, width, channels))
    cotan_q = d_out.reshape((steps, width, channels))

    group = 32 // (2 * hd)
    chunks = steps // group
    lr_shape = (n, chunks, group * 2 * hd, width)
    group3 = 16 // hd
    chunks3 = steps // group3
    tri_shape = (n, chunks3, group3 * hd, width)
    crop_rows = n * row_count
    relayout = [
        pltpu.VMEM((width // LANES, n * steps * 2 * hd, LANES), F32),
        pltpu.VMEM(((crop + LANES - 1) // LANES, crop_rows, LANES), F32),
        pltpu.VMEM((width // LANES, n * steps * hd, LANES), F32),
    ]
    grad_rows = 4 * hidden + hidden + channels
    part = grad_rows // n
    if fused:
        buffers = [(n, splits * chunks, group * 2 * hd // splits, width)] * 4 + [tri_shape] * 4
        rest = [
            pltpu.VMEM((2, hd, crop_rows, crop), BF16),
            pltpu.VMEM((steps, width, channels), BF16),
            pltpu.VMEM((steps, width, channels), BF16),
            pltpu.VMEM((grad_rows, channels), F32),
            pltpu.VMEM((group, 4 * hidden, width), BF16),
            pltpu.VMEM((grad_rows, channels), BF16),
            pltpu.VMEM((n, part, channels), BF16),
            pltpu.VMEM((n, part, channels), BF16),
        ]
        update, d_pair, total = pl.pallas_call(
            functools.partial(fused_kernel, n, hd, fold, splits, chunks, group, chunks3, group3, 1.0 / crop),
            name="triangle_update",
            out_shape=(
                jax.ShapeDtypeStruct((steps, width, channels), BF16),
                jax.ShapeDtypeStruct((steps, width, channels), BF16),
                jax.ShapeDtypeStruct((n, part, channels), F32),
            ),
            in_specs=[VMEM] * 7,
            out_specs=(VMEM, VMEM, VMEM),
            scratch_shapes=[pltpu.VMEM(shape, BF16) for shape in buffers]
            + relayout
            + rest
            + [DMA((splits * chunks, n))] * 4
            + [DMA((chunks3, n))] * 4
            + [DMA((n,))] * 4,
            compiler_params=pltpu.CompilerParams(
                collective_id=3, has_side_effects=True, vmem_limit_bytes=54 * 1024 * 1024
            ),
        )(pair_q, cotan_q, pmask, w_perm_t, w_perm, w_gate, w_out)
    else:
        normed, lr = pl.pallas_call(
            functools.partial(first_kernel, n, chunks, group),
            name="project_and_send",
            out_shape=(
                jax.ShapeDtypeStruct((steps, width, channels), BF16),
                jax.ShapeDtypeStruct(lr_shape, BF16),
            ),
            in_specs=[VMEM] * 3,
            out_specs=(VMEM, ANY),
            scratch_shapes=[pltpu.VMEM(lr_shape, BF16), DMA((chunks, n)), DMA((chunks, n)), DMA],
            compiler_params=params(0),
        )(pair_q, pmask, w_perm_t)

        tri, sides = pl.pallas_call(
            functools.partial(triangle_kernel, n, hd, fold),
            name="triangle",
            out_shape=(
                jax.ShapeDtypeStruct(tri_shape, BF16),
                jax.ShapeDtypeStruct((2, hd, crop_rows, crop), BF16),
            ),
            in_specs=[VMEM],
            out_specs=(VMEM, VMEM),
            scratch_shapes=relayout,
            compiler_params=pltpu.CompilerParams(vmem_limit_bytes=50 * 1024 * 1024),
        )(lr)

        update, dgp, grads, d_tri = pl.pallas_call(
            functools.partial(middle_kernel, n, chunks3, group3),
            name="gate_and_back",
            out_shape=(
                jax.ShapeDtypeStruct((steps, width, channels), BF16),
                jax.ShapeDtypeStruct((steps, width, channels), BF16),
                jax.ShapeDtypeStruct((hidden + channels, channels), F32),
                jax.ShapeDtypeStruct(tri_shape, BF16),
            ),
            in_specs=[ANY] + [VMEM] * 4,
            out_specs=(VMEM, VMEM, VMEM, ANY),
            scratch_shapes=[
                pltpu.VMEM(tri_shape, BF16),
                pltpu.VMEM(tri_shape, BF16),
                DMA((chunks3, n)),
                DMA((chunks3, n)),
                DMA((chunks3, n)),
                DMA((chunks3, n)),
                DMA((2,)),
            ],
            compiler_params=params(1),
        )(tri, normed, cotan_q, w_gate, w_out)

        dlr = pl.pallas_call(
            functools.partial(triangle_back_kernel, n, hd, fold),
            name="triangle_back",
            out_shape=jax.ShapeDtypeStruct(lr_shape, BF16),
            in_specs=[VMEM, VMEM],
            out_specs=VMEM,
            scratch_shapes=relayout,
            compiler_params=pltpu.CompilerParams(vmem_limit_bytes=50 * 1024 * 1024),
        )(d_tri, sides)

        d_pair, total = pl.pallas_call(
            functools.partial(last_kernel, n, chunks, group, 1.0 / crop),
            name="pair_gradient",
            out_shape=(
                jax.ShapeDtypeStruct((steps, width, channels), BF16),
                jax.ShapeDtypeStruct((n, part, channels), F32),
            ),
            in_specs=[ANY] + [VMEM] * 8,
            out_specs=(VMEM, VMEM),
            scratch_shapes=[
                pltpu.VMEM(lr_shape, BF16),
                pltpu.VMEM((grad_rows, channels), F32),
                pltpu.VMEM((n, part, channels), F32),
                DMA((chunks, n)),
                DMA((chunks, n)),
                DMA((n,)),
                DMA((n,)),
                DMA((n,)),
                DMA((n,)),
                DMA,
            ],
            compiler_params=params(2),
        )(dlr, pair_q, normed, dgp, pmask, w_perm_t, w_perm, w_gate, grads)

    total = total.reshape((grad_rows, channels))
    total_in = total[: 4 * hidden].reshape((2, n, splits, 2, hd // splits, channels)).transpose((5, 3, 0, 1, 2, 4))
    total_in = total_in.reshape((channels, 4 * hidden))
    return (
        update.reshape(pair.shape),
        d_pair.reshape(pair.shape),
        total_in,
        total[5 * hidden :],
        total[4 * hidden : 5 * hidden],
    )


def solution(mesh):
    in_specs = (
        P(("groups", "dap"), None, None),
        P(("groups", "dap"), None, None),
        P("groups"),
        P(),
        P(),
        P(),
    )
    out_specs = (
        P(("groups", "dap"), None, None),
        P(("groups", "dap"), None, None),
        P("groups", None),
        P("groups", None),
        P("groups", None),
    )
    body = functools.partial(shards, mesh.shape[AXIS])
    return jax.shard_map(body, mesh=mesh, in_specs=in_specs, out_specs=out_specs, check_vma=False)
```
